256 devices in a mesh: ctx: 64 (over x, z, core), head: 4 (over y).
Axes of the slice: x: 4, y: 4, z: 8, core: 2. Of those that a mesh axis runs over, the one named last changes fastest.
Arguments:
- queries: bfloat16 [8192, 6144], P('ctx', 'head'), may hold values from -2 to 2
- keys_in: bfloat16 [8192, 6144], P('ctx', 'head'), may hold values from -2 to 2
- values_in: bfloat16 [8192, 6144], P('ctx', 'head'), may hold values from -26 to 26
- out_grad: bfloat16 [8192, 6144], P('ctx', 'head'), may hold values from -6 to 6
- gated_fading_logarithms: float32 [64, 8192], P('head', 'ctx'), may hold values from -1 to 0
- norm_gain: float32 [6144], P('head'), may hold values from 0.1 to 1.9
Outputs:
- grad_queries: bfloat16 [8192, 6144], P('ctx', 'head')
- grad_keys: bfloat16 [8192, 6144], P('ctx', 'head')
- grad_values: bfloat16 [8192, 6144], P('ctx', 'head')
The draws below stay inside these ranges and needn't reach their ends.
All inputs are finite; a program needn't handle non-finite values.
Results may differ from the reference program's by a relative error of at most 0.0051.
Values sent between devices are 32-bit elements; how exact they have to be, the bound alone decides.
No kernel may reach another device: no remote copies, remote signals or barrier semaphores. Data moves between devices by JAX's collectives and lax.ppermute only.
A program may use at most 256 MiB of HBM per device.

```python
import jax
import jax.numpy as jnp
from jax import lax

HEADS = 64
HEAD_DIM = 96
D = 6144
TOK_DEV = 128
BLOCK = 128
TOKENS = 8192


def draw_gated_fading_logarithms(key, part):
    key = jax.random.fold_in(key, 11)
    keys = jax.random.split(key, 7)
    slow_count = HEADS // 2
    order = jax.random.permutation(keys[0], HEADS)
    slow = order < slow_count
    slow_rate = jax.random.uniform(keys[1], (HEADS,), jnp.float32, 0.1, 0.7) / TOKENS
    fast_rate = jax.random.uniform(keys[2], (HEADS,), jnp.float32, 1.0 / 50, 1.0 / 30)
    base = jnp.where(slow, slow_rate, fast_rate)
    shards = TOKENS // TOK_DEV
    shard_factor = jnp.exp(jax.random.uniform(keys[3], (HEADS, shards), jnp.float32, -0.69, 0.69))
    shard_factor = jnp.repeat(shard_factor, TOK_DEV, axis=1)
    rough = jnp.exp(jax.random.uniform(keys[4], (HEADS, TOKENS), jnp.float32, -0.4, 0.4))
    fading_speed = base[:, None] * shard_factor * rough
    element_slots = jax.random.randint(keys[5], (HEADS, 3), 0, TOKENS)
    fading_falls = jnp.log(jax.random.uniform(keys[6], (HEADS, 3), jnp.float32, 0.65, 0.8))
    element_locations = lax.broadcasted_iota(jnp.int32, (HEADS, 3, TOKENS), 2)
    fading_spikes = jnp.sum(jnp.where(element_locations == element_slots[:, :, None], fading_falls[:, :, None], 0.0), axis=1)
    return (fading_spikes - fading_speed).astype(jnp.float32)


def draw_values_in(key, part):
    key = jax.random.fold_in(key, 23)
    first, second = jax.random.split(key, 2)
    ladder = jnp.arange(HEADS, dtype=jnp.float32) / max(HEADS - 1, 1)
    jitter = jnp.exp(jax.random.uniform(first, (HEADS,), jnp.float32, -0.35, 0.35))
    scales = 3.0 ** ladder * jitter
    entries = jnp.clip(jax.random.normal(second, (TOKENS, HEADS, HEAD_DIM), jnp.float32), -6.0, 6.0)
    return (entries * scales[None, :, None]).reshape(TOKENS, HEADS * HEAD_DIM).astype(jnp.bfloat16)


def block_levels(stream_key, dims, cuts, low, largest):
    loudness = 1.0
    for axis_at, blocks in cuts:
        heights = jax.random.uniform(jax.random.fold_in(jax.random.fold_in(stream_key, 6), axis_at), (blocks,), jnp.float32, low / len(cuts), largest / len(cuts))
        loudness = loudness * jnp.repeat(jnp.exp(heights), dims[axis_at] // blocks).reshape((-1,) + (1,) * (len(dims) - 1 - axis_at))
    return loudness


def gaussian(key, dims, scale, reach, pieces=(), kind=jnp.bfloat16):
    factor_of = block_levels(key, dims, pieces, -0.22, 0.18) if pieces else 1.0
    drawn = jax.random.normal(key, dims, jnp.float32) * scale * factor_of
    return jnp.minimum(jnp.maximum(drawn, -reach), reach).astype(kind)


def setup_inputs(seed: int = 0) -> dict:
    streams_of = jax.random.split(jax.random.key(seed), 7)
    queries = gaussian(streams_of[0], (TOKENS, D), (HEAD_DIM ** -0.25), 2.0, ((0, 64), (1, 4)))
    keys_in = gaussian(streams_of[1], (TOKENS, D), (HEAD_DIM ** -0.25), 2.0, ((0, 64), (1, 4)))
    values_in = draw_values_in(jax.random.fold_in(streams_of[6], 71), 0)
    out_grad = gaussian(streams_of[3], (TOKENS, D), 1.0, 6.0, ((0, 64), (1, 4)))
    gated_fading_logarithms = draw_gated_fading_logarithms(jax.random.fold_in(streams_of[6], 71), 0)
    norm_gain = jnp.clip(1.0 + 0.18 * jax.random.normal(streams_of[5], (D,), jnp.float32), 0.1, 1.9)
    return dict(queries=queries, keys_in=keys_in, values_in=values_in, out_grad=out_grad, gated_fading_logarithms=gated_fading_logarithms, norm_gain=norm_gain)


PRECISE_MODE = lax.Precision.HIGHEST

def block_weight(decays):
    accum = jnp.cumsum(decays, axis=1)
    span = decays.shape[1]
    rows = lax.broadcasted_iota(jnp.int32, (span, span), 0)
    cols = lax.broadcasted_iota(jnp.int32, (span, span), 1)
    lower = (cols <= rows)[None]
    spread = accum[:, :, None] - accum[:, None, :]
    weight = jnp.where(lower, jnp.exp(jnp.where(lower, spread, 0.0)), 0.0)
    return (accum, weight)

def reference(queries, keys_in, values_in, out_grad, gated_fading_logarithms, norm_gain):
    count = TOKENS // BLOCK

    def split(x):
        return x.reshape(count, BLOCK, HEADS, HEAD_DIM)
    qs, ks, vs, ys = (split(queries), split(keys_in), split(values_in), split(out_grad))
    decays = gated_fading_logarithms.reshape(HEADS, count, BLOCK).transpose(1, 0, 2)
    gain = norm_gain.astype(jnp.float32).reshape(HEADS, HEAD_DIM)

    def forward(running_state, inputs):
        qb, kb, vb, yb, gb = inputs
        queries_wide = qb.astype(jnp.float32)
        keys_wide = kb.astype(jnp.float32)
        values_wide = vb.astype(jnp.float32)
        accum, weight = block_weight(gb)
        last_position = accum[:, -1]
        qk_weights = (jnp.einsum('thd,shd->hts', queries_wide, keys_wide) * weight).astype(jnp.bfloat16)
        inner = jnp.einsum('hts,shd->thd', qk_weights.astype(jnp.float32), values_wide)
        block_start = jnp.exp(accum).T[:, :, None]
        outer_product = block_start * jnp.einsum('zmo,mol->zml', queries_wide, running_state, precision=PRECISE_MODE)
        attention = inner + outer_product
        squares = lax.optimization_barrier(jnp.sum(attention * attention, axis=(1, 2)))
        root = jnp.sqrt(squares / (HEADS * HEAD_DIM) + 1e-05)
        scaled = gain[None] * yb.astype(jnp.float32)
        crossed = lax.optimization_barrier(jnp.sum(scaled * attention, axis=(1, 2)))
        factor = crossed / (HEADS * HEAD_DIM * root ** 3)
        norm_back = (scaled / root[:, None, None] - attention * factor[:, None, None]).astype(jnp.bfloat16)
        back_grad_wide = norm_back.astype(jnp.float32)
        back_weights = (jnp.einsum('thd,shd->hts', back_grad_wide, values_wide) * weight).astype(jnp.bfloat16)
        query_gradient = jnp.einsum('hts,shd->thd', back_weights.astype(jnp.float32), keys_wide)
        query_gradient = query_gradient + block_start * jnp.einsum('bsp,snp->bsn', back_grad_wide, running_state, precision=PRECISE_MODE)
        tail_decay = jnp.exp(last_position[:, None] - accum).T[:, :, None]
        block_state_matrix = jnp.einsum('rpz,rpb->pzb', keys_wide * tail_decay, values_wide, precision=PRECISE_MODE)
        new_state = jnp.exp(last_position)[:, None, None] * running_state + block_state_matrix
        return (new_state, (norm_back, query_gradient.astype(jnp.bfloat16)))
    empty = jnp.zeros((HEADS, HEAD_DIM, HEAD_DIM), jnp.float32)
    final_state, (backs, grad_qs) = lax.scan(forward, empty, (qs, ks, vs, ys, decays))

    def backward(carried_state, inputs):
        qb, kb, vb, db, gb = inputs
        queries_wide = qb.astype(jnp.float32)
        keys_wide = kb.astype(jnp.float32)
        values_wide = vb.astype(jnp.float32)
        decay_wide = db.astype(jnp.float32)
        accum, weight = block_weight(gb)
        last_position = accum[:, -1]
        qk_weights = (jnp.einsum('thd,shd->hts', queries_wide, keys_wide) * weight).astype(jnp.bfloat16)
        back_weights = (jnp.einsum('thd,shd->hts', decay_wide, values_wide) * weight).astype(jnp.bfloat16)
        tail_decay = jnp.exp(last_position[:, None] - accum).T[:, :, None]
        key_gradient = jnp.einsum('hts,thd->shd', back_weights.astype(jnp.float32), queries_wide)
        key_gradient = key_gradient + tail_decay * jnp.einsum('baz,aiz->bai', values_wide, carried_state, precision=PRECISE_MODE)
        value_gradient = jnp.einsum('hts,thd->shd', qk_weights.astype(jnp.float32), decay_wide)
        value_gradient = value_gradient + tail_decay * jnp.einsum('tpa,pao->tpo', keys_wide, carried_state, precision=PRECISE_MODE)
        block_start = jnp.exp(accum).T[:, :, None]
        updated_carried_state = jnp.exp(last_position)[:, None, None] * carried_state + jnp.einsum('rua,rus->uas', queries_wide * block_start, decay_wide, precision=PRECISE_MODE)
        return (updated_carried_state, (key_gradient.astype(jnp.bfloat16), value_gradient.astype(jnp.bfloat16)))
    first_carry, (grad_ks, grad_vs) = lax.scan(backward, empty, (qs, ks, vs, backs, decays), reverse=True)
    shape = (TOKENS, HEADS * HEAD_DIM)
    return (grad_qs.reshape(shape), grad_ks.reshape(shape), grad_vs.reshape(shape))
```

```python
import jax
import jax.numpy as jnp
from jax import lax
from jax.experimental import pallas as pl
from jax.experimental.pallas import tpu as pltpu
from jax.sharding import Mesh, PartitionSpec as P

HEADS = 64
HEAD_DIM = 96
TOKENS = 128
LOCAL_HEADS = 16
HALF = 8
WIDTH = LOCAL_HEADS * HEAD_DIM
LANES = 128
PACK = 72
CHIPS = 32
PART = 18
FWD_PART = 20
ROWS = LOCAL_HEADS * PACK
HALF_ROWS = HALF * PACK
VMEM = 48 * 1024 * 1024

F32 = jnp.float32
BF16 = jnp.bfloat16

START = (0, 0, 128, 256)
SPAN = (128, 256, 256, 128)
FIRST = (0, 96, 64, 32)
FREE = (3, 2, 1, 0)


def lanes_of(shape):
    return lax.broadcasted_iota(jnp.int32, shape, len(shape) - 1)


def rows_of(shape):
    return lax.broadcasted_iota(jnp.int32, shape, len(shape) - 2)


def dot_nn(a, b):
    return lax.dot_general(a, b, (((1,), (0,)), ((), ())), preferred_element_type=F32)


def dot_nt(a, b):
    return lax.dot_general(a, b, (((1,), (1,)), ((), ())), preferred_element_type=F32)


def two(x):
    high = x.astype(BF16)
    return high, (x - high.astype(F32)).astype(BF16)


def head_tiles(value, g, j, masked):
    part = value[:, 384 * g + START[j] : 384 * g + START[j] + SPAN[j]]
    if masked:
        lane = lanes_of(part.shape)
        part = jnp.where((lane >= FIRST[j]) & (lane < FIRST[j] + HEAD_DIM), part, jnp.zeros_like(part))
    return part


def merge(tiles):
    return tiles if tiles.shape[1] == LANES else tiles[:, :LANES] + tiles[:, LANES:]


def pack(square, j):
    lane = lanes_of((24, LANES))
    free = lane // 32 == FREE[j]
    extra = square[PACK:]
    others = [c for c in range(4) if c != FREE[j]]
    return [
        jnp.where(free, pltpu.roll(extra, (32 * (FREE[j] - c)) % LANES, 1), square[24 * i : 24 * i + 24])
        for i, c in enumerate(others)
    ]


def unpack(packed, j):
    lane = lanes_of((24, LANES))
    others = [c for c in range(4) if c != FREE[j]]
    extra = jnp.zeros((24, LANES), F32)
    for i, c in enumerate(others):
        moved = pltpu.roll(packed[24 * i : 24 * i + 24], (32 * (c - FREE[j])) % LANES, 1)
        extra = jnp.where(lane // 32 == c, moved, extra)
    return jnp.concatenate([packed, extra], axis=0)


def spread(square, j):
    lane = lanes_of(square.shape)
    zero = jnp.zeros_like(square)
    if j == 0:
        tiles = (jnp.where(lane < 96, square, zero), zero, zero)
    elif j == 1:
        tiles = (jnp.where(lane >= 96, square, zero), jnp.where(lane < 64, square, zero), zero)
    elif j == 2:
        tiles = (zero, jnp.where(lane >= 64, square, zero), jnp.where(lane < 32, square, zero))
    else:
        tiles = (zero, zero, jnp.where(lane >= 32, square, zero))
    return jnp.concatenate(tiles, axis=1)


def block_diagonal(ref, g):
    rows = []
    for j in range(4):
        h = 4 * g + j
        rows.append(spread(unpack(ref[PACK * h : PACK * h + PACK, :], j), j))
    return two(jnp.concatenate(rows, axis=0))


def running(logs):
    lane = lanes_of(logs.shape)
    total = logs
    for k in (1, 2, 4, 8, 16, 32, 64):
        total = total + jnp.where(lane >= k, pltpu.roll(total, k, 1), 0.0)
    return total


def columns(rows):
    filler = jnp.zeros((LANES - rows.shape[0], LANES), F32)
    return jnp.concatenate([rows, filler], axis=0).T


def wide_column(cols, h):
    return jnp.broadcast_to(cols[:, h : h + 1], (TOKENS, LANES))


def group_columns(cols, g):
    lane = lanes_of((TOKENS, LANES))
    c = [wide_column(cols, 4 * g + j) for j in range(4)]
    return jnp.concatenate(
        [jnp.where(lane < 96, c[0], c[1]), jnp.where(lane < 64, c[1], c[2]), jnp.where(lane < 32, c[2], c[3])],
        axis=1,
    )


def weight_of(accum, cols, h):
    row = accum[h : h + 1, :]
    spread_by = wide_column(cols, h) - row
    shape = (TOKENS, LANES)
    keep = lanes_of(shape) <= rows_of(shape)
    return jnp.where(keep, jnp.exp(jnp.where(keep, spread_by, 0.0)), 0.0)


def weight_turned(accum, cols, h):
    spread_by = accum[h : h + 1, :] - wide_column(cols, h)
    shape = (TOKENS, LANES)
    keep = rows_of(shape) <= lanes_of(shape)
    return jnp.where(keep, jnp.exp(jnp.where(keep, spread_by, 0.0)), 0.0)


def outer_states(left_ref, scale, right, out_ref):
    for g in range(4):
        turned = left_ref[:, 384 * g : 384 * g + 384].astype(F32).T
        for j in range(4):
            h = 4 * g + j
            high, low = two(turned[96 * j : 96 * j + 96, :] * scale[h : h + 1, :])
            both = dot_nn(jnp.concatenate([high, low], axis=0), head_tiles(right, g, j, True))
            square = merge(both[:96] + both[96:])
            for i, piece in enumerate(pack(square, j)):
                out_ref[PACK * h + 24 * i : PACK * h + 24 * i + 24, :] = piece


def state_kernel(k_ref, v_ref, logs_ref, x_ref):
    accum = running(logs_ref[...])
    last = accum[:, LANES - 1 :]
    outer_states(k_ref, jnp.exp(last - accum), v_ref, x_ref)
    x_ref[ROWS : ROWS + LOCAL_HEADS, :] = jnp.broadcast_to(jnp.exp(last), (LOCAL_HEADS, LANES))


def combine_forward_kernel(core_ref, own_ref, got_ref, out_ref, own_decay_ref, got_decay_ref):
    core = core_ref[0]
    own_decay_ref[...] = own_ref[ROWS : ROWS + LOCAL_HEADS, :]
    got_decay_ref[...] = got_ref[ROWS : ROWS + LOCAL_HEADS, :]
    first = core == 0
    at = pl.multiple_of(ROWS + HALF * core, 8)
    own_decay = own_ref[pl.ds(at, HALF), :]
    got_decay = got_ref[pl.ds(at, HALF), :]
    late_decay = jnp.where(first, got_decay, own_decay)
    both_decay = own_decay * got_decay
    for h in range(HALF):
        at = pl.multiple_of(HALF_ROWS * core + PACK * h, 8)
        own = own_ref[pl.ds(at, PACK), :]
        got = got_ref[pl.ds(at, PACK), :]
        early = jnp.where(first, own, got)
        late = jnp.where(first, got, own)
        total = early * late_decay[h : h + 1, :] + late
        for quarter in range(4):
            to = FWD_PART * (4 * h + quarter)
            out_ref[to : to + PART, :] = total[PART * quarter : PART * quarter + PART, :]
            out_ref[to + PART : to + FWD_PART, :] = jnp.broadcast_to(both_decay[h : h + 1, :], (2, LANES))


def combine_backward_kernel(core_ref, own_ref, got_ref, own_decay_ref, got_decay_ref, out_ref):
    core = core_ref[0]
    first = core == 0
    at = pl.multiple_of(HALF * core, 8)
    early_decay = jnp.where(first, own_decay_ref[pl.ds(at, HALF), :], got_decay_ref[pl.ds(at, HALF), :])
    for h in range(HALF):
        at = pl.multiple_of(HALF_ROWS * core + PACK * h, 8)
        own = own_ref[pl.ds(at, PACK), :]
        got = got_ref[pl.ds(at, PACK), :]
        early = jnp.where(first, own, got)
        late = jnp.where(first, got, own)
        out_ref[PACK * h : PACK * h + PACK, :] = late * early_decay[h : h + 1, :] + early


def scan_forward_kernel(in_ref, out_ref, decay_ref):
    state = jnp.zeros((PART, LANES), F32)
    for c in range(CHIPS):
        out_ref[PART * c : PART * c + PART, :] = state
        at = FWD_PART * c
        decay = in_ref[at + PART : at + PART + 1, :]
        decay_ref[c : c + 1, :] = decay
        state = state * decay + in_ref[at : at + PART, :]


def scan_backward_kernel(in_ref, decay_ref, out_ref):
    state = jnp.zeros((PART, LANES), F32)
    for c in reversed(range(CHIPS)):
        out_ref[PART * c : PART * c + PART, :] = state
        state = state * decay_ref[c : c + 1, :] + in_ref[PART * c : PART * c + PART, :]


def finish_states(mine, other, add_ref, decay, own_ref, got_ref, out_ref):
    for h in range(LOCAL_HEADS):
        at = PACK * (h % HALF)
        own = own_ref[at : at + PACK, :]
        got = got_ref[at : at + PACK, :]
        state = jnp.where(mine, own, got) if h < HALF else jnp.where(mine, got, own)
        stepped = state * decay[h : h + 1, :] + add_ref[PACK * h : PACK * h + PACK, :]
        out_ref[PACK * h : PACK * h + PACK, :] = jnp.where(other, stepped, state)


def inner_kernel(q_ref, k_ref, v_ref, logs_ref, inner_ref):
    accum = running(logs_ref[...])
    cols = columns(accum)
    for g in range(4):
        tiles = [None] * 3
        for j in range(4):
            h = 4 * g + j
            scores = dot_nt(head_tiles(q_ref, g, j, True), head_tiles(k_ref, g, j, False))
            weights = (scores * weight_of(accum, cols, h)).astype(BF16)
            part = dot_nn(weights, head_tiles(v_ref, g, j, True))
            for i in range(SPAN[j] // LANES):
                t = START[j] // LANES + i
                piece = part[:, LANES * i : LANES * i + LANES]
                tiles[t] = piece if tiles[t] is None else tiles[t] + piece
        for t in range(3):
            inner_ref[:, 384 * g + LANES * t : 384 * g + LANES * t + LANES] = tiles[t]


def attention_kernel(
    core_ref, q_ref, y_ref, gain_ref, logs_ref, inner_ref, own_ref, got_ref, got_state_ref, o_ref, state_ref, sums_ref
):
    core = core_ref[0]
    decay = got_state_ref[ROWS : ROWS + LOCAL_HEADS, :]
    finish_states(core == 0, core == 1, got_state_ref, decay, own_ref, got_ref, state_ref)
    start = jnp.exp(columns(running(logs_ref[...])))
    squares = jnp.zeros((TOKENS, LANES), F32)
    crossed = jnp.zeros((TOKENS, LANES), F32)
    for g in range(4):
        high, low = block_diagonal(state_ref, g)
        at = slice(384 * g, 384 * g + 384)
        q = q_ref[:, at]
        attention = inner_ref[:, at] + group_columns(start, g) * (dot_nn(q, high) + dot_nn(q, low))
        o_ref[:, at] = attention
        scaled = gain_ref[:, at] * y_ref[:, at].astype(F32)
        both = scaled * attention
        square = attention * attention
        for t in range(3):
            squares = squares + square[:, LANES * t : LANES * t + LANES]
            crossed = crossed + both[:, LANES * t : LANES * t + LANES]
    sums_ref[0:1, :] = jnp.sum(squares.T, axis=0, keepdims=True)
    sums_ref[1:2, :] = jnp.sum(crossed.T, axis=0, keepdims=True)


def norm_kernel(q_ref, y_ref, gain_ref, logs_ref, o_ref, sums_ref, back_ref, c_ref):
    accum = running(logs_ref[...])
    root = jnp.sqrt(sums_ref[0:1, :] / (HEADS * HEAD_DIM) + 1e-05)
    factor = sums_ref[1:2, :] / (HEADS * HEAD_DIM * root * root * root)
    cols = columns(jnp.concatenate([1.0 / root, factor], axis=0))
    inverse = jnp.broadcast_to(cols[:, 0:1], (TOKENS, 384))
    factor = jnp.broadcast_to(cols[:, 1:2], (TOKENS, 384))
    for g in range(4):
        at = slice(384 * g, 384 * g + 384)
        scaled = gain_ref[:, at] * y_ref[:, at].astype(F32)
        back_ref[:, at] = (scaled * inverse - o_ref[:, at] * factor).astype(BF16)
    outer_states(q_ref, jnp.exp(accum), back_ref, c_ref)


def middle_kernel(q_ref, k_ref, v_ref, back_ref, logs_ref, state_ref, gq_ref, gk_ref, gv_ref):
    accum = running(logs_ref[...])
    cols = columns(accum)
    start = jnp.exp(cols)
    for g in range(4):
        high, low = block_diagonal(state_ref, g)
        at = slice(384 * g, 384 * g + 384)
        back = back_ref[:, at]
        gq = group_columns(start, g) * (dot_nt(back, high) + dot_nt(back, low))
        gq = [gq[:, LANES * t : LANES * t + LANES] for t in range(3)]
        gk = [None] * 3
        gv = [None] * 3
        for j in range(4):
            h = 4 * g + j
            q = head_tiles(q_ref, g, j, True)
            k = head_tiles(k_ref, g, j, True)
            v = head_tiles(v_ref, g, j, False)
            d = head_tiles(back_ref, g, j, True)
            weight = weight_of(accum, cols, h)
            turned = weight_turned(accum, cols, h)
            weights = (dot_nt(d, v) * weight).astype(BF16)
            weights_t = (dot_nt(v, d) * turned).astype(BF16)
            qk_t = (dot_nt(k, q) * turned).astype(BF16)
            to_q = dot_nn(weights, k)
            to_k = dot_nn(weights_t, q)
            to_v = dot_nn(qk_t, d)
            for i in range(SPAN[j] // LANES):
                t = START[j] // LANES + i
                lane = slice(LANES * i, LANES * i + LANES)
                gq[t] = gq[t] + to_q[:, lane]
                gk[t] = to_k[:, lane] if gk[t] is None else gk[t] + to_k[:, lane]
                gv[t] = to_v[:, lane] if gv[t] is None else gv[t] + to_v[:, lane]
        for t in range(3):
            lane = slice(384 * g + LANES * t, 384 * g + LANES * t + LANES)
            gq_ref[:, lane] = gq[t].astype(BF16)
            gk_ref[:, lane] = gk[t]
            gv_ref[:, lane] = gv[t]


def last_kernel(
    core_ref, k_ref, v_ref, logs_ref, gk0_ref, gv0_ref, own_ref, got_ref, got_c_ref, got_decay_ref, gk_ref, gv_ref, carry_ref
):
    core = core_ref[0]
    finish_states(core == 0, core == 0, got_c_ref, got_decay_ref[...], own_ref, got_ref, carry_ref)
    accum = running(logs_ref[...])
    tail = columns(jnp.exp(accum[:, LANES - 1 :] - accum))
    for g in range(4):
        high, low = block_diagonal(carry_ref, g)
        at = slice(384 * g, 384 * g + 384)
        k = k_ref[:, at]
        v = v_ref[:, at]
        wide = group_columns(tail, g)
        gk_ref[:, at] = (gk0_ref[:, at] + wide * (dot_nt(v, high) + dot_nt(v, low))).astype(BF16)
        gv_ref[:, at] = (gv0_ref[:, at] + wide * (dot_nn(k, high) + dot_nn(k, low))).astype(BF16)


def call(kernel, outs, smem, *args, scratch=(), flops=0):
    specs = []
    for i, arg in enumerate(args):
        if i < smem:
            specs.append(pl.BlockSpec(memory_space=pltpu.SMEM))
        else:
            specs.append(pl.BlockSpec(memory_space=pltpu.VMEM))
    shapes = [jax.ShapeDtypeStruct(s, d) for s, d in outs]
    moved = sum(a.size * a.dtype.itemsize for a in args) + sum(s.size * s.dtype.itemsize for s in shapes)
    out = pl.pallas_call(
        kernel,
        out_shape=shapes,
        in_specs=specs,
        out_specs=[pl.BlockSpec(memory_space=pltpu.VMEM)] * len(shapes),
        scratch_shapes=scratch,
        compiler_params=pltpu.CompilerParams(vmem_limit_bytes=VMEM),
        cost_estimate=pl.CostEstimate(flops=flops, bytes_accessed=moved, transcendentals=0),
        name=kernel.__name__,
    )(*args)
    return out[0] if len(out) == 1 else out


SWAP = [(0, 1), (1, 0)]
CHIP_AXES = ("x", "z")


def swap(value):
    return lax.ppermute(value, "core", SWAP)


def exchange(value):
    flat = lax.all_to_all(value.reshape(-1), CHIP_AXES, 0, 0, tiled=True)
    return flat.reshape(value.shape)


def local(q, k, v, y, logs, gain):
    core = lax.axis_index("core").astype(jnp.int32).reshape(1)
    gain = gain.reshape(1, WIDTH)
    wide = (TOKENS, WIDTH)
    x = call(state_kernel, [((ROWS + LOCAL_HEADS, LANES), F32)], 0, k, v, logs, flops=2 * 10**8)
    got_x = swap(x)
    decay = ((LOCAL_HEADS, LANES), F32)
    payload, own_decay, got_decay = call(
        combine_forward_kernel, [((CHIPS * FWD_PART, LANES), F32), decay, decay], 1, core, x, got_x
    )
    payload = exchange(payload)
    inner = call(inner_kernel, [(wide, F32)], 0, q, k, v, logs, flops=4 * 10**8)
    entering, decays = call(scan_forward_kernel, [((HALF_ROWS, LANES), F32), ((CHIPS, LANES), F32)], 0, payload)
    entering = exchange(entering)
    got_entering = swap(entering)
    attention, state, sums = call(
        attention_kernel,
        [(wide, F32), ((ROWS, LANES), F32), ((2, LANES), F32)],
        1, core, q, y, gain, logs, inner, entering, got_entering, got_x,
        flops=4 * 10**8,
    )
    sums = lax.psum(sums, "head")
    back, c = call(norm_kernel, [(wide, BF16), ((ROWS, LANES), F32)], 0, q, y, gain, logs, attention, sums, flops=2 * 10**8)
    got_c = swap(c)
    payload = call(
        combine_backward_kernel, [((HALF_ROWS, LANES), F32)], 1, core, c, got_c, own_decay, got_decay
    )
    payload = exchange(payload)
    gq, gk0, gv0 = call(
        middle_kernel, [(wide, BF16), (wide, F32), (wide, F32)], 0, q, k, v, back, logs, state, flops=10**9
    )
    leaving = call(scan_backward_kernel, [((HALF_ROWS, LANES), F32)], 0, payload, decays)
    leaving = exchange(leaving)
    got_leaving = swap(leaving)
    gk, gv = call(
        last_kernel,
        [(wide, BF16), (wide, BF16)],
        1, core, k, v, logs, gk0, gv0, leaving, got_leaving, got_c, got_decay,
        scratch=[pltpu.VMEM((ROWS, LANES), F32)],
        flops=4 * 10**8,
    )
    return gq, gk, gv


def solution(mesh):
    grid = Mesh(mesh.devices.reshape(4, 8, 2, 4), ("x", "z", "core", "head"))
    tokens = ("x", "z", "core")
    rows = P(tokens, "head")
    return jax.shard_map(
        local,
        mesh=grid,
        in_specs=(rows, rows, rows, rows, P("head", tokens), P("head")),
        out_specs=(rows, rows, rows),
        check_vma=False,
    )
```

```python
import jax
import jax.numpy as jnp
from jax import lax
from jax.experimental import pallas as pl
from jax.experimental.pallas import tpu as pltpu
from jax.sharding import Mesh, PartitionSpec as P

HEADS = 64
HEAD_DIM = 96
TOKENS = 128
LOCAL_HEADS = 16
HALF = 8
WIDTH = LOCAL_HEADS * HEAD_DIM
LANES = 128
PACK = 72
CHIPS = 32
PART = 18
FWD_PART = 20
ROWS = LOCAL_HEADS * PACK
HALF_ROWS = HALF * PACK
VMEM = 12 * 1024 * 1024

F32 = jnp.float32
BF16 = jnp.bfloat16

START = (0, 0, 128, 256)
SPAN = (128, 256, 256, 128)
FIRST = (0, 96, 64, 32)
FREE = (3, 2, 1, 0)


def lanes_of(shape):
    return lax.broadcasted_iota(jnp.int32, shape, len(shape) - 1)


def rows_of(shape):
    return lax.broadcasted_iota(jnp.int32, shape, len(shape) - 2)


def dot_nn(a, b):
    return lax.dot_general(a, b, (((1,), (0,)), ((), ())), preferred_element_type=F32)


def dot_nt(a, b):
    return lax.dot_general(a, b, (((1,), (1,)), ((), ())), preferred_element_type=F32)


def two(x):
    high = x.astype(BF16)
    return high, (x - high.astype(F32)).astype(BF16)


def head_tiles(value, g, j, masked):
    part = value[:, 384 * g + START[j] : 384 * g + START[j] + SPAN[j]]
    if masked:
        lane = lanes_of(part.shape)
        part = jnp.where((lane >= FIRST[j]) & (lane < FIRST[j] + HEAD_DIM), part, jnp.zeros_like(part))
    return part


def merge(tiles):
    return tiles if tiles.shape[1] == LANES else tiles[:, :LANES] + tiles[:, LANES:]


def pack(square, j):
    lane = lanes_of((24, LANES))
    free = lane // 32 == FREE[j]
    extra = square[PACK:]
    others = [c for c in range(4) if c != FREE[j]]
    return [
        jnp.where(free, pltpu.roll(extra, (32 * (FREE[j] - c)) % LANES, 1), square[24 * i : 24 * i + 24])
        for i, c in enumerate(others)
    ]


def unpack(packed, j):
    lane = lanes_of((24, LANES))
    others = [c for c in range(4) if c != FREE[j]]
    extra = jnp.zeros((24, LANES), F32)
    for i, c in enumerate(others):
        moved = pltpu.roll(packed[24 * i : 24 * i + 24], (32 * (c - FREE[j])) % LANES, 1)
        extra = jnp.where(lane // 32 == c, moved, extra)
    return jnp.concatenate([packed, extra], axis=0)


def spread(square, j):
    lane = lanes_of(square.shape)
    zero = jnp.zeros_like(square)
    if j == 0:
        tiles = (jnp.where(lane < 96, square, zero), zero, zero)
    elif j == 1:
        tiles = (jnp.where(lane >= 96, square, zero), jnp.where(lane < 64, square, zero), zero)
    elif j == 2:
        tiles = (zero, jnp.where(lane >= 64, square, zero), jnp.where(lane < 32, square, zero))
    else:
        tiles = (zero, zero, jnp.where(lane >= 32, square, zero))
    return jnp.concatenate(tiles, axis=1)


def block_diagonal(ref, g):
    rows = []
    for j in range(4):
        h = 4 * g + j
        rows.append(spread(unpack(ref[PACK * h : PACK * h + PACK, :], j), j))
    return two(jnp.concatenate(rows, axis=0))


def running(logs):
    lane = lanes_of(logs.shape)
    total = logs
    for k in (1, 2, 4, 8, 16, 32, 64):
        total = total + jnp.where(lane >= k, pltpu.roll(total, k, 1), 0.0)
    return total


def columns(rows):
    filler = jnp.zeros((LANES - rows.shape[0], LANES), F32)
    return jnp.concatenate([rows, filler], axis=0).T


def wide_column(cols, h):
    return jnp.broadcast_to(cols[:, h : h + 1], (TOKENS, LANES))


def group_columns(cols, g):
    lane = lanes_of((TOKENS, LANES))
    c = [wide_column(cols, 4 * g + j) for j in range(4)]
    return jnp.concatenate(
        [jnp.where(lane < 96, c[0], c[1]), jnp.where(lane < 64, c[1], c[2]), jnp.where(lane < 32, c[2], c[3])],
        axis=1,
    )


def weight_of(accum, cols, h):
    row = accum[h : h + 1, :]
    spread_by = wide_column(cols, h) - row
    shape = (TOKENS, LANES)
    keep = lanes_of(shape) <= rows_of(shape)
    return jnp.where(keep, jnp.exp(jnp.where(keep, spread_by, 0.0)), 0.0)


def weight_turned(accum, cols, h):
    spread_by = accum[h : h + 1, :] - wide_column(cols, h)
    shape = (TOKENS, LANES)
    keep = rows_of(shape) <= lanes_of(shape)
    return jnp.where(keep, jnp.exp(jnp.where(keep, spread_by, 0.0)), 0.0)


def turn_and_scale(left_ref, scale, g):
    turned = left_ref[:, 384 * g : 384 * g + 384].astype(F32).T
    return [
        jnp.concatenate(two(turned[96 * j : 96 * j + 96, :] * scale[4 * g + j : 4 * g + j + 1, :]), axis=0)
        for j in range(4)
    ]


def outer_states(left, right, out_ref):
    for g in range(4):
        for j in range(4):
            h = 4 * g + j
            both = dot_nn(left(h), head_tiles(right, g, j, True))
            square = merge(both[:96] + both[96:])
            for i, piece in enumerate(pack(square, j)):
                out_ref[PACK * h + 24 * i : PACK * h + 24 * i + 24, :] = piece


def state_kernel(kv_ref, logs_ref, x_ref):
    accum = running(logs_ref[...])
    last = accum[:, LANES - 1 :]
    tail = jnp.exp(last - accum)
    turned = [both for g in range(4) for both in turn_and_scale(kv_ref[:TOKENS], tail, g)]
    outer_states(lambda h: turned[h], kv_ref[TOKENS:], x_ref)
    x_ref[ROWS : ROWS + LOCAL_HEADS, :] = jnp.broadcast_to(jnp.exp(last), (LOCAL_HEADS, LANES))


def combine_forward_kernel(core_ref, own_ref, got_ref, out_ref, own_decay_ref, got_decay_ref):
    core = core_ref[0]
    own_decay_ref[...] = own_ref[ROWS : ROWS + LOCAL_HEADS, :]
    got_decay_ref[...] = got_ref[ROWS : ROWS + LOCAL_HEADS, :]
    first = core == 0
    at = pl.multiple_of(ROWS + HALF * core, 8)
    own_decay = own_ref[pl.ds(at, HALF), :]
    got_decay = got_ref[pl.ds(at, HALF), :]
    late_decay = jnp.where(first, got_decay, own_decay)
    both_decay = own_decay * got_decay
    for h in range(HALF):
        at = pl.multiple_of(HALF_ROWS * core + PACK * h, 8)
        own = own_ref[pl.ds(at, PACK), :]
        got = got_ref[pl.ds(at, PACK), :]
        early = jnp.where(first, own, got)
        late = jnp.where(first, got, own)
        total = early * late_decay[h : h + 1, :] + late
        for quarter in range(4):
            to = FWD_PART * (4 * h + quarter)
            out_ref[to : to + PART, :] = total[PART * quarter : PART * quarter + PART, :]
            out_ref[to + PART : to + FWD_PART, :] = jnp.broadcast_to(both_decay[h : h + 1, :], (2, LANES))


def combine_backward_kernel(core_ref, own_ref, got_ref, own_decay_ref, got_decay_ref, out_ref):
    core = core_ref[0]
    first = core == 0
    at = pl.multiple_of(HALF * core, 8)
    early_decay = jnp.where(first, own_decay_ref[pl.ds(at, HALF), :], got_decay_ref[pl.ds(at, HALF), :])
    for h in range(HALF):
        at = pl.multiple_of(HALF_ROWS * core + PACK * h, 8)
        own = own_ref[pl.ds(at, PACK), :]
        got = got_ref[pl.ds(at, PACK), :]
        early = jnp.where(first, own, got)
        late = jnp.where(first, got, own)
        out_ref[PACK * h : PACK * h + PACK, :] = late * early_decay[h : h + 1, :] + early


def turned_bits(c):
    return sum(((c >> b) & 1) << (4 - b) for b in range(5))


def scan_forward_kernel(in_ref, out_ref, decay_ref):
    state = jnp.zeros((PART, LANES), F32)
    for c in range(CHIPS):
        place = turned_bits(c)
        out_ref[PART * place : PART * place + PART, :] = state
        at = FWD_PART * place
        decay = in_ref[at + PART : at + PART + 1, :]
        decay_ref[c : c + 1, :] = decay
        state = state * decay + in_ref[at : at + PART, :]


def scan_backward_kernel(in_ref, decay_ref, after_ref, out_ref):
    state = jnp.zeros((PART, LANES), F32)
    for c in reversed(range(CHIPS)):
        at = PART * turned_bits(c)
        out_ref[at : at + PART, :] = state
        state = state * decay_ref[c : c + 1, :] + in_ref[at : at + PART, :]


def finish_states(g, mine, other, add_ref, decay, own_ref, got_ref, out_ref):
    for h in range(4 * g, 4 * g + 4):
        at = PACK * (h % HALF)
        own = own_ref[at : at + PACK, :]
        got = got_ref[at : at + PACK, :]
        state = jnp.where(mine, own, got) if h < HALF else jnp.where(mine, got, own)
        stepped = state * decay[h : h + 1, :] + add_ref[PACK * h : PACK * h + PACK, :]
        out_ref[PACK * h : PACK * h + PACK, :] = jnp.where(other, stepped, state)


def add_tiles(tiles, part, j):
    for i in range(SPAN[j] // LANES):
        t = START[j] // LANES + i
        piece = part[:, LANES * i : LANES * i + LANES]
        tiles[t] = piece if tiles[t] is None else tiles[t] + piece


def inner_kernel(q_ref, k_ref, v_ref, logs_ref, inner_ref):
    accum = running(logs_ref[...])
    cols = columns(accum)
    for g in range(4):
        tiles = [None] * 3
        for j in range(4):
            h = 4 * g + j
            scores = dot_nt(head_tiles(q_ref, g, j, True), head_tiles(k_ref, g, j, False))
            weights = (scores * weight_of(accum, cols, h)).astype(BF16)
            add_tiles(tiles, dot_nn(weights, head_tiles(v_ref, g, j, True)), j)
        for t in range(3):
            inner_ref[:, 384 * g + LANES * t : 384 * g + LANES * t + LANES] = tiles[t]


def attention_kernel(
    core_ref, q_ref, y_ref, gain_ref, logs_ref, inner_ref, own_ref, got_ref, got_state_ref, o_ref, state_ref, sums_ref
):
    core = core_ref[0]
    decay = got_state_ref[ROWS : ROWS + LOCAL_HEADS, :]
    start = jnp.exp(columns(running(logs_ref[...])))
    squares = jnp.zeros((TOKENS, LANES), F32)
    crossed = jnp.zeros((TOKENS, LANES), F32)
    for g in range(4):
        finish_states(g, core == 0, core == 1, got_state_ref, decay, own_ref, got_ref, state_ref)
        high, low = block_diagonal(state_ref, g)
        at = slice(384 * g, 384 * g + 384)
        q = q_ref[:, at]
        attention = inner_ref[:, at] + group_columns(start, g) * (dot_nn(q, high) + dot_nn(q, low))
        o_ref[:, at] = attention
        scaled = gain_ref[:, at] * y_ref[:, at].astype(F32)
        both = scaled * attention
        square = attention * attention
        for t in range(3):
            squares = squares + square[:, LANES * t : LANES * t + LANES]
            crossed = crossed + both[:, LANES * t : LANES * t + LANES]
    sums_ref[0:1, :] = jnp.sum(squares.T, axis=0, keepdims=True)
    sums_ref[1:2, :] = jnp.sum(crossed.T, axis=0, keepdims=True)


def norm_kernel(q_ref, y_ref, gain_ref, logs_ref, o_ref, sums_0, sums_1, sums_2, sums_3, back_ref, c_ref):
    accum = running(logs_ref[...])
    sums = (sums_0[...] + sums_1[...]) + (sums_2[...] + sums_3[...])
    root = jnp.sqrt(sums[0:1, :] / (HEADS * HEAD_DIM) + 1e-05)
    factor = sums[1:2, :] / (HEADS * HEAD_DIM * root * root * root)
    cols = columns(jnp.concatenate([1.0 / root, factor], axis=0))
    inverse = jnp.broadcast_to(cols[:, 0:1], (TOKENS, 384))
    factor = jnp.broadcast_to(cols[:, 1:2], (TOKENS, 384))
    for g in range(4):
        at = slice(384 * g, 384 * g + 384)
        scaled = gain_ref[:, at] * y_ref[:, at].astype(F32)
        back_ref[:, at] = (scaled * inverse - o_ref[:, at] * factor).astype(BF16)
    scale = jnp.exp(accum)
    turned = [both for g in range(4) for both in turn_and_scale(q_ref, scale, g)]
    outer_states(lambda h: turned[h], back_ref, c_ref)


def middle_kernel(q_ref, k_ref, v_ref, back_ref, logs_ref, state_ref, gq_ref, gk_ref, done_ref):
    accum = running(logs_ref[...])
    done_ref[...] = accum[:8]
    cols = columns(accum)
    start = jnp.exp(cols)
    for g in range(4):
        high, low = block_diagonal(state_ref, g)
        at = slice(384 * g, 384 * g + 384)
        back = back_ref[:, at]
        gq = group_columns(start, g) * (dot_nt(back, high) + dot_nt(back, low))
        gq = [gq[:, LANES * t : LANES * t + LANES] for t in range(3)]
        gk = [None] * 3
        for j in range(4):
            h = 4 * g + j
            q = head_tiles(q_ref, g, j, True)
            k = head_tiles(k_ref, g, j, True)
            v = head_tiles(v_ref, g, j, False)
            d = head_tiles(back_ref, g, j, True)
            weights = (dot_nt(d, v) * weight_of(accum, cols, h)).astype(BF16)
            weights_t = (dot_nt(v, d) * weight_turned(accum, cols, h)).astype(BF16)
            add_tiles(gq, dot_nn(weights, k), j)
            add_tiles(gk, dot_nn(weights_t, q), j)
        for t in range(3):
            lane = slice(384 * g + LANES * t, 384 * g + LANES * t + LANES)
            gq_ref[:, lane] = gq[t].astype(BF16)
            gk_ref[:, lane] = gk[t]


def values_kernel(q_ref, k_ref, back_ref, logs_ref, gv_ref):
    accum = running(logs_ref[...])
    cols = columns(accum)
    for g in range(4):
        gv = [None] * 3
        for j in range(4):
            h = 4 * g + j
            scores = dot_nt(head_tiles(k_ref, g, j, True), head_tiles(q_ref, g, j, False))
            weights = (scores * weight_turned(accum, cols, h)).astype(BF16)
            add_tiles(gv, dot_nn(weights, head_tiles(back_ref, g, j, True)), j)
        for t in range(3):
            gv_ref[:, 384 * g + LANES * t : 384 * g + LANES * t + LANES] = gv[t]


def last_kernel(
    core_ref, k_ref, v_ref, logs_ref, gk0_ref, gv0_ref, own_ref, got_ref, got_c_ref, got_decay_ref,
    gk_hbm, gv_hbm, carry_ref, gk_ref, gv_ref, sems,
):
    core = core_ref[0]
    decay = got_decay_ref[...]
    accum = running(logs_ref[...])
    tail = columns(jnp.exp(accum[:, LANES - 1 :] - accum))
    copies = []
    for g in range(4):
        finish_states(g, core == 0, core == 0, got_c_ref, decay, own_ref, got_ref, carry_ref)
        high, low = block_diagonal(carry_ref, g)
        at = slice(384 * g, 384 * g + 384)
        k = k_ref[:, at]
        v = v_ref[:, at]
        wide = group_columns(tail, g)
        gk_ref[:, at] = (gk0_ref[:, at] + wide * (dot_nt(v, high) + dot_nt(v, low))).astype(BF16)
        gv_ref[:, at] = (gv0_ref[:, at] + wide * (dot_nn(k, high) + dot_nn(k, low))).astype(BF16)
        for i, (src, dst) in enumerate(((gk_ref, gk_hbm), (gv_ref, gv_hbm))):
            copy = pltpu.make_async_copy(src.at[:, at], dst.at[:, at], sems.at[2 * g + i])
            copy.start()
            copies.append(copy)
    for copy in copies:
        copy.wait()


def call(kernel, outs, smem, *args, hbm_in=(), hbm_out=(), scratch=(), flops=0, vmem=VMEM):
    specs = []
    for i, arg in enumerate(args):
        space = pltpu.SMEM if i < smem else pltpu.HBM if i in hbm_in else pltpu.VMEM
        specs.append(pl.BlockSpec(memory_space=space))
    shapes = [jax.ShapeDtypeStruct(s, d) for s, d in outs]
    moved = sum(a.size * a.dtype.itemsize for a in args) + sum(s.size * s.dtype.itemsize for s in shapes)
    out = pl.pallas_call(
        kernel,
        out_shape=shapes,
        in_specs=specs,
        out_specs=[pl.BlockSpec(memory_space=pltpu.HBM if i in hbm_out else pltpu.VMEM) for i in range(len(shapes))],
        scratch_shapes=scratch,
        compiler_params=pltpu.CompilerParams(vmem_limit_bytes=vmem),
        cost_estimate=pl.CostEstimate(flops=flops, bytes_accessed=moved, transcendentals=0),
        name=kernel.__name__,
    )(*args)
    return out[0] if len(out) == 1 else out


SWAP = [(0, 1), (1, 0)]
CHIP_BITS = ("xh", "xl", "zh", "zm", "zl")


def swap(value):
    return lax.ppermute(value, "core", SWAP)


def exchange(value):
    parts = value.reshape(CHIPS, -1, 2, LANES)
    return lax.all_to_all(parts, CHIP_BITS[::-1], 0, 0, tiled=True).reshape(value.shape)


def others(value):
    return [lax.ppermute(value, "head", [(i, (i + k) % 4) for i in range(4)]) for k in (1, 2, 3)]


def local(q, k, v, y, logs, gain):
    core = lax.axis_index("core").astype(jnp.int32).reshape(1)
    gain = gain.reshape(1, WIDTH)
    wide = (TOKENS, WIDTH)
    narrow = pltpu.VMEM(wide, BF16)
    decay = ((LOCAL_HEADS, LANES), F32)
    x = call(state_kernel, [((ROWS + LOCAL_HEADS, LANES), F32)], 0, jnp.concatenate([k, v]), logs, flops=10**9)
    got_x = swap(x)
    payload, own_decay, got_decay = call(
        combine_forward_kernel, [((CHIPS * FWD_PART, LANES), F32), decay, decay], 1, core, x, got_x
    )
    payload = exchange(payload)
    token = ((8, LANES), F32)
    inner = call(inner_kernel, [(wide, F32)], 0, q, k, v, logs, flops=2 * 10**9)
    entering, decays = call(scan_forward_kernel, [((HALF_ROWS, LANES), F32), ((CHIPS, LANES), F32)], 0, payload)
    entering = exchange(entering)
    got_entering = swap(entering)
    attention, state, sums = call(
        attention_kernel,
        [(wide, F32), ((ROWS, LANES), F32), ((2, LANES), F32)],
        1, core, q, y, gain, logs, inner, entering, got_entering, got_x,
        flops=10**9,
    )
    back, c = call(
        norm_kernel,
        [(wide, BF16), ((ROWS, LANES), F32)],
        0, q, y, gain, logs, attention, sums, *others(sums),
        flops=10**9,
    )
    got_c = swap(c)
    payload = call(
        combine_backward_kernel, [((HALF_ROWS, LANES), F32)], 1, core, c, got_c, own_decay, got_decay
    )
    payload = exchange(payload)
    gq, gk0, middle_done = call(
        middle_kernel, [(wide, BF16), (wide, F32), token], 0, q, k, v, back, logs, state, flops=4 * 10**9
    )
    leaving = call(scan_backward_kernel, [((HALF_ROWS, LANES), F32)], 0, payload, decays, middle_done)
    leaving = exchange(leaving)
    got_leaving = swap(leaving)
    gv0 = call(values_kernel, [(wide, F32)], 0, q, k, back, logs, flops=2 * 10**9)
    gk, gv = call(
        last_kernel,
        [(wide, BF16), (wide, BF16)],
        1, core, k, v, logs, gk0, gv0, leaving, got_leaving, got_c, got_decay,
        hbm_out=(0, 1),
        scratch=[pltpu.VMEM((ROWS, LANES), F32), narrow, narrow, pltpu.SemaphoreType.DMA((8,))],
        flops=2 * 10**9,
    )
    return gq, gk, gv


def solution(mesh):
    tokens = (*CHIP_BITS, "core")
    grid = Mesh(mesh.devices.reshape(2, 2, 2, 2, 2, 2, 4), (*tokens, "head"))
    rows = P(tokens, "head")
    return jax.shard_map(
        local,
        mesh=grid,
        in_specs=(rows, rows, rows, rows, P("head", tokens), P("head")),
        out_specs=(rows, rows, rows),
        check_vma=False,
    )
```

```python
import jax
import jax.numpy as jnp
from jax import lax
from jax.experimental import pallas as pl
from jax.experimental.pallas import tpu as pltpu
from jax.sharding import Mesh, PartitionSpec as P

HEADS = 64
HEAD_DIM = 96
TOKENS = 128
LOCAL_HEADS = 16
HALF = 8
WIDTH = LOCAL_HEADS * HEAD_DIM
LANES = 128
PACK = 72
CHIPS = 32
PART = 18
FWD_PART = 20
ROWS = LOCAL_HEADS * PACK
HALF_ROWS = HALF * PACK
VMEM = 12 * 1024 * 1024

F32 = jnp.float32
BF16 = jnp.bfloat16

START = (0, 0, 128, 256)
SPAN = (128, 256, 256, 128)
FIRST = (0, 96, 64, 32)
FREE = (3, 2, 1, 0)


def lanes_of(shape):
    return lax.broadcasted_iota(jnp.int32, shape, len(shape) - 1)


def rows_of(shape):
    return lax.broadcasted_iota(jnp.int32, shape, len(shape) - 2)


def dot_nn(a, b):
    return lax.dot_general(a, b, (((1,), (0,)), ((), ())), preferred_element_type=F32)


def dot_nt(a, b):
    return lax.dot_general(a, b, (((1,), (1,)), ((), ())), preferred_element_type=F32)


def two(x):
    high = x.astype(BF16)
    return high, (x - high.astype(F32)).astype(BF16)


def at_lanes(base, start, size):
    return pl.ds(base + start if isinstance(base, int) else pl.multiple_of(base + start, LANES), size)


def head_tiles(value, g, j, masked):
    part = value[:, at_lanes(384 * g, START[j], SPAN[j])]
    if masked:
        lane = lanes_of(part.shape)
        part = jnp.where((lane >= FIRST[j]) & (lane < FIRST[j] + HEAD_DIM), part, jnp.zeros_like(part))
    return part


def merge(tiles):
    return tiles if tiles.shape[1] == LANES else tiles[:, :LANES] + tiles[:, LANES:]


def pack(square, j):
    lane = lanes_of((24, LANES))
    free = lane // 32 == FREE[j]
    extra = square[PACK:]
    others = [c for c in range(4) if c != FREE[j]]
    return [
        jnp.where(free, pltpu.roll(extra, (32 * (FREE[j] - c)) % LANES, 1), square[24 * i : 24 * i + 24])
        for i, c in enumerate(others)
    ]


def unpack(packed, j):
    lane = lanes_of((24, LANES))
    others = [c for c in range(4) if c != FREE[j]]
    extra = jnp.zeros((24, LANES), F32)
    for i, c in enumerate(others):
        moved = pltpu.roll(packed[24 * i : 24 * i + 24], (32 * (c - FREE[j])) % LANES, 1)
        extra = jnp.where(lane // 32 == c, moved, extra)
    return jnp.concatenate([packed, extra], axis=0)


def spread(square, j):
    lane = lanes_of(square.shape)
    zero = jnp.zeros_like(square)
    if j == 0:
        tiles = (jnp.where(lane < 96, square, zero), zero)
    elif j == 1:
        tiles = (jnp.where(lane >= 96, square, zero), jnp.where(lane < 64, square, zero))
    elif j == 2:
        tiles = (jnp.where(lane >= 64, square, zero), jnp.where(lane < 32, square, zero))
    else:
        tiles = (zero, jnp.where(lane >= 32, square, zero))
    return jnp.concatenate(tiles, axis=1)


def pair_states(ref, g, pair):
    parts = []
    for j in (2 * pair, 2 * pair + 1):
        h = 4 * g + j
        parts.append([spread(part, j) for part in two(unpack(ref[PACK * h : PACK * h + PACK, :], j))])
    zero = jnp.zeros((64, 256), BF16)
    out = []
    for first, second in zip(*parts):
        rows = [first, second, zero] if pair == 0 else [zero, first, second]
        out.append(jnp.concatenate(rows, axis=0))
    return out


def times_states(values, pairs, dot):
    left, right = (
        dot(values[:, LANES * p : LANES * p + 256], pairs[p][0])
        + dot(values[:, LANES * p : LANES * p + 256], pairs[p][1])
        for p in range(2)
    )
    return jnp.concatenate([left[:, :LANES], left[:, LANES:] + right[:, :LANES], right[:, LANES:]], axis=1)


def running(logs):
    high = logs.astype(BF16)
    rest = logs - high.astype(F32)
    middle = rest.astype(BF16)
    low = (rest - middle.astype(F32)).astype(BF16)
    shape = (LANES, LANES)
    upto = jnp.where(rows_of(shape) <= lanes_of(shape), 1.0, 0.0).astype(BF16)
    return dot_nn(low, upto) + dot_nn(middle, upto) + dot_nn(high, upto)


def columns(rows):
    filler = jnp.zeros((LANES - rows.shape[0], LANES), F32)
    return jnp.concatenate([rows, filler], axis=0).T


def wide_column(cols, h):
    return jnp.broadcast_to(cols[:, h : h + 1], (TOKENS, LANES))


def group_columns(cols, g):
    lane = lanes_of((TOKENS, LANES))
    c = [wide_column(cols, 4 * g + j) for j in range(4)]
    return jnp.concatenate(
        [jnp.where(lane < 96, c[0], c[1]), jnp.where(lane < 64, c[1], c[2]), jnp.where(lane < 32, c[2], c[3])],
        axis=1,
    )


def weight_of(accum, cols, h):
    row = accum[h : h + 1, :]
    spread_by = wide_column(cols, h) - row
    shape = (TOKENS, LANES)
    keep = lanes_of(shape) <= rows_of(shape)
    return jnp.where(keep, jnp.exp(jnp.where(keep, spread_by, 0.0)), 0.0)


def weight_turned(accum, cols, h):
    spread_by = accum[h : h + 1, :] - wide_column(cols, h)
    shape = (TOKENS, LANES)
    keep = rows_of(shape) <= lanes_of(shape)
    return jnp.where(keep, jnp.exp(jnp.where(keep, spread_by, 0.0)), 0.0)


def outer_states(half, left_ref, scale, right_ref, out_ref):
    for i in range(2):
        g = 2 * half + i
        turned = left_ref[:, at_lanes(384 * g, 0, 384)].astype(F32).T
        for j in range(4):
            h = 4 * i + j
            left = jnp.concatenate(two(turned[96 * j : 96 * j + 96, :] * scale[h : h + 1, :]), axis=0)
            both = dot_nn(left, head_tiles(right_ref, g, j, True))
            square = merge(both[:96] + both[96:])
            for n, piece in enumerate(pack(square, j)):
                out_ref[PACK * h + 24 * n : PACK * h + 24 * n + 24, :] = piece


def half_rows(ref, half):
    return ref[pl.ds(pl.multiple_of(HALF * half, HALF), HALF), :]


def state_half(half, kv_ref, accum_ref, out_ref):
    accum = half_rows(accum_ref, half)
    last = jnp.broadcast_to(accum[:, LANES - 1 :], (HALF, LANES))
    out_ref[HALF_ROWS : HALF_ROWS + HALF, :] = jnp.exp(last)
    keys, values = kv_ref.at[pl.ds(0, TOKENS)], kv_ref.at[pl.ds(TOKENS, TOKENS)]
    outer_states(half, keys, jnp.exp(last - accum), values, out_ref)


def state_send_kernel(core_ref, kv_ref, logs_ref, out_ref, accum_ref):
    accum_ref[...] = running(logs_ref[...])
    state_half(1 - core_ref[0], kv_ref, accum_ref, out_ref)


def state_keep_kernel(core_ref, kv_ref, accum_ref, out_ref):
    state_half(core_ref[0], kv_ref, accum_ref, out_ref)


def combine_forward_kernel(core_ref, own_ref, got_ref, out_ref):
    first = core_ref[0] == 0
    own_decay = own_ref[HALF_ROWS : HALF_ROWS + HALF, :]
    got_decay = got_ref[HALF_ROWS : HALF_ROWS + HALF, :]
    late_decay = jnp.where(first, got_decay, own_decay)
    both_decay = own_decay * got_decay
    for h in range(HALF):
        own = own_ref[PACK * h : PACK * h + PACK, :]
        got = got_ref[PACK * h : PACK * h + PACK, :]
        early = jnp.where(first, own, got)
        late = jnp.where(first, got, own)
        total = early * late_decay[h : h + 1, :] + late
        for quarter in range(4):
            to = FWD_PART * (4 * h + quarter)
            out_ref[to : to + PART, :] = total[PART * quarter : PART * quarter + PART, :]
            out_ref[to + PART : to + FWD_PART, :] = jnp.broadcast_to(both_decay[h : h + 1, :], (2, LANES))


def combine_backward_kernel(core_ref, own_ref, got_ref, own_x_ref, got_x_ref, out_ref):
    first = core_ref[0] == 0
    at = slice(HALF_ROWS, HALF_ROWS + HALF)
    early_decay = jnp.where(first, own_x_ref[at, :], got_x_ref[at, :])
    for h in range(HALF):
        own = own_ref[PACK * h : PACK * h + PACK, :]
        got = got_ref[PACK * h : PACK * h + PACK, :]
        early = jnp.where(first, own, got)
        late = jnp.where(first, got, own)
        out_ref[PACK * h : PACK * h + PACK, :] = late * early_decay[h : h + 1, :] + early


def turned_bits(c):
    return sum(((c >> b) & 1) << (4 - b) for b in range(5))


def scan_forward_kernel(in_ref, out_ref, decay_ref):
    state = jnp.zeros((PART, LANES), F32)
    for c in range(CHIPS):
        place = turned_bits(c)
        out_ref[PART * place : PART * place + PART, :] = state
        at = FWD_PART * place
        decay = in_ref[at + PART : at + PART + 1, :]
        decay_ref[c : c + 1, :] = decay
        state = state * decay + in_ref[at : at + PART, :]


def scan_backward_kernel(in_ref, decay_ref, after_ref, out_ref):
    state = jnp.zeros((PART, LANES), F32)
    for c in reversed(range(CHIPS)):
        at = PART * turned_bits(c)
        out_ref[at : at + PART, :] = state
        state = state * decay_ref[c : c + 1, :] + in_ref[at : at + PART, :]


def step_kernel(core_ref, stepping, state_ref, add_ref, decay_ref, out_ref):
    steps = core_ref[0] == stepping
    for h in range(HALF):
        at = slice(PACK * h, PACK * h + PACK)
        state = state_ref[at, :]
        stepped = state * decay_ref[HALF_ROWS + h : HALF_ROWS + h + 1, :] + add_ref[at, :]
        out_ref[at, :] = jnp.where(steps, stepped, state)


def step_forward_kernel(core_ref, state_ref, x_ref, out_ref):
    step_kernel(core_ref, 0, state_ref, x_ref, x_ref, out_ref)


def step_backward_kernel(core_ref, state_ref, c_ref, x_ref, out_ref):
    step_kernel(core_ref, 1, state_ref, c_ref, x_ref, out_ref)


def finish_states(g, core, late, own_ref, got_ref, add_ref, decay_ref, out_ref):
    half = g // 2
    for h in range(4 * g, 4 * g + 4):
        i = h % HALF
        own = own_ref[PACK * i : PACK * i + PACK, :]
        got = got_ref[PACK * i : PACK * i + PACK, :]
        if half == late:
            own = own * decay_ref[HALF_ROWS + i : HALF_ROWS + i + 1, :] + add_ref[PACK * i : PACK * i + PACK, :]
        out_ref[PACK * h : PACK * h + PACK, :] = jnp.where(core == half, own, got)


def add_tiles(tiles, part, j):
    for i in range(SPAN[j] // LANES):
        t = START[j] // LANES + i
        piece = part[:, LANES * i : LANES * i + LANES]
        tiles[t] = piece if tiles[t] is None else tiles[t] + piece


def inner_kernel(q_ref, k_ref, v_ref, accum_ref, inner_ref, start_ref, tail_ref):
    accum = accum_ref[...]
    cols = columns(accum)
    start_ref[...] = jnp.exp(cols)
    tail_ref[...] = columns(jnp.exp(accum[:, LANES - 1 :] - accum))
    for g in range(4):
        tiles = [None] * 3
        for j in range(4):
            h = 4 * g + j
            scores = dot_nt(head_tiles(q_ref, g, j, True), head_tiles(k_ref, g, j, False))
            weights = (scores * weight_of(accum, cols, h)).astype(BF16)
            add_tiles(tiles, dot_nn(weights, head_tiles(v_ref, g, j, True)), j)
        for t in range(3):
            inner_ref[:, 384 * g + LANES * t : 384 * g + LANES * t + LANES] = tiles[t]


def attention_kernel(
    core_ref, q_ref, y_ref, gain_ref, start_ref, inner_ref, own_ref, got_ref, got_x_ref,
    o_ref, state_ref, sums_ref,
):
    core = core_ref[0]
    start = start_ref[...]
    squares = jnp.zeros((TOKENS, LANES), F32)
    crossed = jnp.zeros((TOKENS, LANES), F32)
    for g in range(4):
        finish_states(g, core, 1, own_ref, got_ref, got_x_ref, got_x_ref, state_ref)
        pairs = [pair_states(state_ref, g, p) for p in range(2)]
        at = slice(384 * g, 384 * g + 384)
        attention = inner_ref[:, at] + group_columns(start, g) * times_states(q_ref[:, at], pairs, dot_nn)
        o_ref[:, at] = attention
        scaled = gain_ref[:, at] * y_ref[:, at].astype(F32)
        both = scaled * attention
        square = attention * attention
        for t in range(3):
            squares = squares + square[:, LANES * t : LANES * t + LANES]
            crossed = crossed + both[:, LANES * t : LANES * t + LANES]
    sums_ref[0:1, :] = jnp.sum(squares.T, axis=0, keepdims=True)
    sums_ref[1:2, :] = jnp.sum(crossed.T, axis=0, keepdims=True)


def norm_kernel(
    core_ref, q_ref, y_ref, gain_ref, accum_ref, o_ref, sums_0, sums_1, sums_2, sums_3, back_ref, c_ref
):
    sums = (sums_0[...] + sums_1[...]) + (sums_2[...] + sums_3[...])
    root = jnp.sqrt(sums[0:1, :] / (HEADS * HEAD_DIM) + 1e-05)
    factor = sums[1:2, :] / (HEADS * HEAD_DIM * root * root * root)
    cols = columns(jnp.concatenate([1.0 / root, factor], axis=0))
    inverse = jnp.broadcast_to(cols[:, 0:1], (TOKENS, 384))
    factor = jnp.broadcast_to(cols[:, 1:2], (TOKENS, 384))
    for g in range(4):
        at = slice(384 * g, 384 * g + 384)
        scaled = gain_ref[:, at] * y_ref[:, at].astype(F32)
        back_ref[:, at] = (scaled * inverse - o_ref[:, at] * factor).astype(BF16)
    half = 1 - core_ref[0]
    outer_states(half, q_ref, jnp.exp(half_rows(accum_ref, half)), back_ref, c_ref)


def carry_keep_kernel(core_ref, q_ref, back_ref, accum_ref, c_ref):
    half = core_ref[0]
    outer_states(half, q_ref, jnp.exp(half_rows(accum_ref, half)), back_ref, c_ref)


def middle_kernel(q_ref, k_ref, v_ref, back_ref, accum_ref, state_ref, gq_ref, gk_ref, done_ref):
    accum = accum_ref[...]
    done_ref[...] = accum[:8]
    cols = columns(accum)
    start = jnp.exp(cols)
    for g in range(4):
        pairs = [pair_states(state_ref, g, p) for p in range(2)]
        at = slice(384 * g, 384 * g + 384)
        gq = group_columns(start, g) * times_states(back_ref[:, at], pairs, dot_nt)
        gq = [gq[:, LANES * t : LANES * t + LANES] for t in range(3)]
        gk = [None] * 3
        for j in range(4):
            h = 4 * g + j
            q = head_tiles(q_ref, g, j, True)
            k = head_tiles(k_ref, g, j, True)
            v = head_tiles(v_ref, g, j, False)
            d = head_tiles(back_ref, g, j, True)
            weights = (dot_nt(d, v) * weight_of(accum, cols, h)).astype(BF16)
            weights_t = (dot_nt(v, d) * weight_turned(accum, cols, h)).astype(BF16)
            add_tiles(gq, dot_nn(weights, k), j)
            add_tiles(gk, dot_nn(weights_t, q), j)
        for t in range(3):
            lane = slice(384 * g + LANES * t, 384 * g + LANES * t + LANES)
            gq_ref[:, lane] = gq[t].astype(BF16)
            gk_ref[:, lane] = gk[t]


def values_kernel(q_ref, k_ref, back_ref, accum_ref, gv_ref):
    accum = accum_ref[...]
    cols = columns(accum)
    for g in range(4):
        gv = [None] * 3
        for j in range(4):
            h = 4 * g + j
            scores = dot_nt(head_tiles(k_ref, g, j, True), head_tiles(q_ref, g, j, False))
            weights = (scores * weight_turned(accum, cols, h)).astype(BF16)
            add_tiles(gv, dot_nn(weights, head_tiles(back_ref, g, j, True)), j)
        for t in range(3):
            gv_ref[:, 384 * g + LANES * t : 384 * g + LANES * t + LANES] = gv[t]


def last_kernel(
    core_ref, k_ref, v_ref, tail_ref, gk0_ref, gv0_ref, own_ref, got_ref, got_c_ref, got_x_ref,
    gk_hbm, gv_hbm, carry_ref, gk_ref, gv_ref, sems,
):
    core = core_ref[0]
    tail = tail_ref[...]
    copies = []
    for g in range(4):
        finish_states(g, core, 0, own_ref, got_ref, got_c_ref, got_x_ref, carry_ref)
        pairs = [pair_states(carry_ref, g, p) for p in range(2)]
        at = slice(384 * g, 384 * g + 384)
        wide = group_columns(tail, g)
        gk_ref[:, at] = (gk0_ref[:, at] + wide * times_states(v_ref[:, at], pairs, dot_nt)).astype(BF16)
        gv_ref[:, at] = (gv0_ref[:, at] + wide * times_states(k_ref[:, at], pairs, dot_nn)).astype(BF16)
        for i, (src, dst) in enumerate(((gk_ref, gk_hbm), (gv_ref, gv_hbm))):
            copy = pltpu.make_async_copy(src.at[:, at], dst.at[:, at], sems.at[2 * g + i])
            copy.start()
            copies.append(copy)
    for copy in copies:
        copy.wait()


def call(kernel, outs, smem, *args, hbm_in=(), hbm_out=(), scratch=(), flops=0, vmem=VMEM):
    specs = []
    for i, arg in enumerate(args):
        space = pltpu.SMEM if i < smem else pltpu.HBM if i in hbm_in else pltpu.VMEM
        specs.append(pl.BlockSpec(memory_space=space))
    shapes = [jax.ShapeDtypeStruct(s, d) for s, d in outs]
    moved = sum(a.size * a.dtype.itemsize for a in args) + sum(s.size * s.dtype.itemsize for s in shapes)
    out = pl.pallas_call(
        kernel,
        out_shape=shapes,
        in_specs=specs,
        out_specs=[pl.BlockSpec(memory_space=pltpu.HBM if i in hbm_out else pltpu.VMEM) for i in range(len(shapes))],
        scratch_shapes=scratch,
        compiler_params=pltpu.CompilerParams(vmem_limit_bytes=vmem),
        cost_estimate=pl.CostEstimate(flops=flops, bytes_accessed=moved, transcendentals=0),
        name=kernel.__name__,
    )(*args)
    return out[0] if len(out) == 1 else out


SWAP = [(0, 1), (1, 0)]
CHIP_BITS = ("xh", "xl", "zh", "zm", "zl")


def swap(value):
    return lax.ppermute(value, "core", SWAP)


def exchange(value):
    parts = value.reshape(CHIPS, -1, 2, LANES)
    return lax.all_to_all(parts, CHIP_BITS[::-1], 0, 0, tiled=True).reshape(value.shape)


def others(value):
    return [lax.ppermute(value, "head", [(i, (i + k) % 4) for i in range(4)]) for k in (1, 2, 3)]


def local(q, k, v, y, logs, gain):
    core = lax.axis_index("core").astype(jnp.int32).reshape(1)
    gain = gain.reshape(1, WIDTH)
    wide = (TOKENS, WIDTH)
    narrow = pltpu.VMEM(wide, BF16)
    half = ((HALF_ROWS, LANES), F32)
    half_decay = ((HALF_ROWS + HALF, LANES), F32)
    rows = ((LOCAL_HEADS, LANES), F32)
    cols = ((TOKENS, LANES), F32)
    kv = jnp.concatenate([k, v])
    kv, logs = lax.optimization_barrier((kv, logs))
    x_send, accum = call(state_send_kernel, [half_decay, rows], 1, core, kv, logs, flops=10**9)
    got_x = swap(x_send)
    x_keep = call(state_keep_kernel, [half_decay], 1, core, kv, accum, flops=10**9)
    payload = call(combine_forward_kernel, [((CHIPS * FWD_PART, LANES), F32)], 1, core, x_keep, got_x)
    payload = exchange(payload)
    inner, start, tail = call(inner_kernel, [(wide, F32), cols, cols], 0, q, k, v, accum, flops=2 * 10**9)
    entering, decays = call(scan_forward_kernel, [half, ((CHIPS, LANES), F32)], 0, payload)
    entering = exchange(entering)
    got_entering = swap(call(step_forward_kernel, [half], 1, core, entering, x_keep))
    attention, state, sums = call(
        attention_kernel,
        [(wide, F32), ((ROWS, LANES), F32), ((2, LANES), F32)],
        1, core, q, y, gain, start, inner, entering, got_entering, got_x,
        flops=10**9,
    )
    back, c_send = call(
        norm_kernel,
        [(wide, BF16), half],
        1, core, q, y, gain, accum, attention, sums, *others(sums),
        flops=10**9,
    )
    got_c = swap(c_send)
    c_keep = call(carry_keep_kernel, [half], 1, core, q, back, accum, flops=10**9)
    payload = call(combine_backward_kernel, [half], 1, core, c_keep, got_c, x_keep, got_x)
    payload = exchange(payload)
    gq, gk0, middle_done = call(
        middle_kernel,
        [(wide, BF16), (wide, F32), ((8, LANES), F32)],
        0, q, k, v, back, accum, state,
        flops=4 * 10**9,
    )
    leaving = call(scan_backward_kernel, [half], 0, payload, decays, middle_done)
    leaving = exchange(leaving)
    got_leaving = swap(call(step_backward_kernel, [half], 1, core, leaving, c_keep, x_keep))
    gv0 = call(values_kernel, [(wide, F32)], 0, q, k, back, accum, flops=2 * 10**9)
    gk, gv = call(
        last_kernel,
        [(wide, BF16), (wide, BF16)],
        1, core, k, v, tail, gk0, gv0, leaving, got_leaving, got_c, got_x,
        hbm_out=(0, 1),
        scratch=[pltpu.VMEM((ROWS, LANES), F32), narrow, narrow, pltpu.SemaphoreType.DMA((8,))],
        flops=2 * 10**9,
    )
    return gq, gk, gv


def solution(mesh):
    tokens = (*CHIP_BITS, "core")
    grid = Mesh(mesh.devices.reshape(2, 2, 2, 2, 2, 2, 4), (*tokens, "head"))
    rows = P(tokens, "head")
    return jax.shard_map(
        local,
        mesh=grid,
        in_specs=(rows, rows, rows, rows, P("head", tokens), P("head")),
        out_specs=(rows, rows, rows),
        check_vma=False,
    )
```

```python
import jax
import jax.numpy as jnp
from jax import lax
from jax.experimental import pallas as pl
from jax.experimental.pallas import tpu as pltpu
from jax.sharding import Mesh, PartitionSpec as P

HEADS = 64
HEAD_DIM = 96
TOKENS = 128
LOCAL_HEADS = 16
HALF = 8
WIDTH = LOCAL_HEADS * HEAD_DIM
LANES = 128
PACK = 72
CHIPS = 32
PART = 18
FWD_PART = 19
ROWS = LOCAL_HEADS * PACK
HALF_ROWS = HALF * PACK
VMEM = 12 * 1024 * 1024

F32 = jnp.float32
BF16 = jnp.bfloat16

START = (0, 0, 128, 256)
SPAN = (128, 256, 256, 128)
FIRST = (0, 96, 64, 32)
FREE = (3, 2, 1, 0)


def lanes_of(shape):
    return lax.broadcasted_iota(jnp.int32, shape, len(shape) - 1)


def rows_of(shape):
    return lax.broadcasted_iota(jnp.int32, shape, len(shape) - 2)


def dot_nn(a, b):
    return lax.dot_general(a, b, (((1,), (0,)), ((), ())), preferred_element_type=F32)


def dot_nt(a, b):
    return lax.dot_general(a, b, (((1,), (1,)), ((), ())), preferred_element_type=F32)


def two(x):
    high = x.astype(BF16)
    return high, (x - high.astype(F32)).astype(BF16)


def at_lanes(base, start, size):
    return pl.ds(base + start if isinstance(base, int) else pl.multiple_of(base + start, LANES), size)


def head_tiles(value, g, j, masked):
    part = value[:, at_lanes(384 * g, START[j], SPAN[j])]
    if masked:
        lane = lanes_of(part.shape)
        part = jnp.where((lane >= FIRST[j]) & (lane < FIRST[j] + HEAD_DIM), part, jnp.zeros_like(part))
    return part


def merge(tiles):
    return tiles if tiles.shape[1] == LANES else tiles[:, :LANES] + tiles[:, LANES:]


def pack(square, j):
    lane = lanes_of((24, LANES))
    free = lane // 32 == FREE[j]
    extra = square[PACK:]
    others = [c for c in range(4) if c != FREE[j]]
    return [
        jnp.where(free, pltpu.roll(extra, (32 * (FREE[j] - c)) % LANES, 1), square[24 * i : 24 * i + 24])
        for i, c in enumerate(others)
    ]


def unpack(packed, j):
    lane = lanes_of((24, LANES))
    others = [c for c in range(4) if c != FREE[j]]
    extra = jnp.zeros((24, LANES), F32)
    for i, c in enumerate(others):
        moved = pltpu.roll(packed[24 * i : 24 * i + 24], (32 * (c - FREE[j])) % LANES, 1)
        extra = jnp.where(lane // 32 == c, moved, extra)
    return jnp.concatenate([packed, extra], axis=0)


def spread(square, j):
    lane = lanes_of(square.shape)
    zero = jnp.zeros_like(square)
    if j == 0:
        tiles = (jnp.where(lane < 96, square, zero), zero)
    elif j == 1:
        tiles = (jnp.where(lane >= 96, square, zero), jnp.where(lane < 64, square, zero))
    elif j == 2:
        tiles = (jnp.where(lane >= 64, square, zero), jnp.where(lane < 32, square, zero))
    else:
        tiles = (zero, jnp.where(lane >= 32, square, zero))
    return jnp.concatenate(tiles, axis=1)


def pair_states(ref, g, pair):
    parts = []
    for j in (2 * pair, 2 * pair + 1):
        h = 4 * g + j
        parts.append([spread(part, j) for part in two(unpack(ref[PACK * h : PACK * h + PACK, :], j))])
    zero = jnp.zeros((64, 256), BF16)
    out = []
    for first, second in zip(*parts):
        rows = [first, second, zero] if pair == 0 else [zero, first, second]
        out.append(jnp.concatenate(rows, axis=0))
    return out


def times_states(values, pairs, dot):
    left, right = (
        dot(values[:, LANES * p : LANES * p + 256], pairs[p][0])
        + dot(values[:, LANES * p : LANES * p + 256], pairs[p][1])
        for p in range(2)
    )
    return jnp.concatenate([left[:, :LANES], left[:, LANES:] + right[:, :LANES], right[:, LANES:]], axis=1)


def running(logs):
    high = logs.astype(BF16)
    rest = logs - high.astype(F32)
    middle = rest.astype(BF16)
    low = (rest - middle.astype(F32)).astype(BF16)
    shape = (LANES, LANES)
    upto = jnp.where(rows_of(shape) <= lanes_of(shape), 1.0, 0.0).astype(BF16)
    return dot_nn(low, upto) + dot_nn(middle, upto) + dot_nn(high, upto)


def columns(rows):
    filler = jnp.zeros((LANES - rows.shape[0], LANES), F32)
    return jnp.concatenate([rows, filler], axis=0).T


def wide_column(cols, h):
    return jnp.broadcast_to(cols[:, h : h + 1], (TOKENS, LANES))


def group_columns(cols, g):
    lane = lanes_of((TOKENS, LANES))
    c = [wide_column(cols, 4 * g + j) for j in range(4)]
    return jnp.concatenate(
        [jnp.where(lane < 96, c[0], c[1]), jnp.where(lane < 64, c[1], c[2]), jnp.where(lane < 32, c[2], c[3])],
        axis=1,
    )


def weight_of(accum, cols, h):
    row = accum[h : h + 1, :]
    spread_by = wide_column(cols, h) - row
    shape = (TOKENS, LANES)
    keep = lanes_of(shape) <= rows_of(shape)
    return jnp.where(keep, jnp.exp(jnp.where(keep, spread_by, 0.0)), 0.0)


def weight_turned(accum, cols, h):
    spread_by = accum[h : h + 1, :] - wide_column(cols, h)
    shape = (TOKENS, LANES)
    keep = rows_of(shape) <= lanes_of(shape)
    return jnp.where(keep, jnp.exp(jnp.where(keep, spread_by, 0.0)), 0.0)


def outer_states(half, left_ref, scale, right_ref, out_ref):
    for i in range(2):
        g = 2 * half + i
        turned = left_ref[:, at_lanes(384 * g, 0, 384)].astype(F32).T
        for j in range(4):
            h = 4 * i + j
            left = jnp.concatenate(two(turned[96 * j : 96 * j + 96, :] * scale[h : h + 1, :]), axis=0)
            both = dot_nn(left, head_tiles(right_ref, g, j, True))
            square = merge(both[:96] + both[96:])
            for n, piece in enumerate(pack(square, j)):
                out_ref[PACK * h + 24 * n : PACK * h + 24 * n + 24, :] = piece


def half_rows(ref, half):
    return ref[pl.ds(pl.multiple_of(HALF * half, HALF), HALF), :]


def state_half(half, kv_ref, accum_ref, out_ref):
    accum = half_rows(accum_ref, half)
    last = jnp.broadcast_to(accum[:, LANES - 1 :], (HALF, LANES))
    out_ref[HALF_ROWS : HALF_ROWS + HALF, :] = jnp.exp(last)
    keys, values = kv_ref.at[pl.ds(0, TOKENS)], kv_ref.at[pl.ds(TOKENS, TOKENS)]
    outer_states(half, keys, jnp.exp(last - accum), values, out_ref)


def state_send_kernel(core_ref, kv_ref, logs_ref, out_ref, accum_ref):
    accum_ref[...] = running(logs_ref[...])
    state_half(1 - core_ref[0], kv_ref, accum_ref, out_ref)


def state_keep_kernel(core_ref, kv_ref, accum_ref, out_ref):
    state_half(core_ref[0], kv_ref, accum_ref, out_ref)


def combine_forward_kernel(core_ref, own_ref, got_ref, out_ref):
    first = core_ref[0] == 0
    own_decay = own_ref[HALF_ROWS : HALF_ROWS + HALF, :]
    got_decay = got_ref[HALF_ROWS : HALF_ROWS + HALF, :]
    late_decay = jnp.where(first, got_decay, own_decay)
    both_decay = own_decay * got_decay
    for h in range(HALF):
        own = own_ref[PACK * h : PACK * h + PACK, :]
        got = got_ref[PACK * h : PACK * h + PACK, :]
        early = jnp.where(first, own, got)
        late = jnp.where(first, got, own)
        total = early * late_decay[h : h + 1, :] + late
        for quarter in range(4):
            to = FWD_PART * (4 * h + quarter)
            out_ref[to : to + PART, :] = total[PART * quarter : PART * quarter + PART, :]
            out_ref[to + PART : to + FWD_PART, :] = both_decay[h : h + 1, :]


def combine_backward_kernel(core_ref, own_ref, got_ref, own_x_ref, got_x_ref, out_ref):
    first = core_ref[0] == 0
    at = slice(HALF_ROWS, HALF_ROWS + HALF)
    early_decay = jnp.where(first, own_x_ref[at, :], got_x_ref[at, :])
    for h in range(HALF):
        own = own_ref[PACK * h : PACK * h + PACK, :]
        got = got_ref[PACK * h : PACK * h + PACK, :]
        early = jnp.where(first, own, got)
        late = jnp.where(first, got, own)
        out_ref[PACK * h : PACK * h + PACK, :] = late * early_decay[h : h + 1, :] + early


def place_of(c):
    return sum(((c >> (4 - CHIP_BITS.index(name))) & 1) << (4 - i) for i, name in enumerate(EXCHANGE))


def scan_forward_kernel(in_ref, out_ref, decay_ref):
    state = jnp.zeros((PART, LANES), F32)
    for c in range(CHIPS):
        place = place_of(c)
        out_ref[PART * place : PART * place + PART, :] = state
        at = FWD_PART * place
        decay = in_ref[at + PART : at + PART + 1, :]
        decay_ref[c : c + 1, :] = decay
        state = state * decay + in_ref[at : at + PART, :]


def scan_backward_kernel(in_ref, decay_ref, after_ref, after_too_ref, out_ref):
    state = jnp.zeros((PART, LANES), F32)
    for c in reversed(range(CHIPS)):
        at = PART * place_of(c)
        out_ref[at : at + PART, :] = state
        state = state * decay_ref[c : c + 1, :] + in_ref[at : at + PART, :]


def step_kernel(core_ref, stepping, state_ref, add_ref, decay_ref, out_ref):
    steps = core_ref[0] == stepping
    for h in range(HALF):
        at = slice(PACK * h, PACK * h + PACK)
        state = state_ref[at, :]
        stepped = state * decay_ref[HALF_ROWS + h : HALF_ROWS + h + 1, :] + add_ref[at, :]
        out_ref[at, :] = jnp.where(steps, stepped, state)


def step_forward_kernel(core_ref, state_ref, x_ref, out_ref):
    step_kernel(core_ref, 0, state_ref, x_ref, x_ref, out_ref)


def step_backward_kernel(core_ref, state_ref, c_ref, x_ref, out_ref):
    step_kernel(core_ref, 1, state_ref, c_ref, x_ref, out_ref)


def own_states(core, late, own_ref, add_ref, decay_ref, out_ref):
    for h in range(HALF):
        at = slice(PACK * h, PACK * h + PACK)
        own = own_ref[at, :]
        stepped = own * decay_ref[HALF_ROWS + h : HALF_ROWS + h + 1, :] + add_ref[at, :]
        out_ref[at, :] = jnp.where(core == late, stepped, own)


def add_tiles(tiles, part, j):
    for i in range(SPAN[j] // LANES):
        t = START[j] // LANES + i
        piece = part[:, LANES * i : LANES * i + LANES]
        tiles[t] = piece if tiles[t] is None else tiles[t] + piece


def keys_of(kv_ref):
    return kv_ref.at[pl.ds(0, TOKENS)]


def values_of(kv_ref):
    return kv_ref.at[pl.ds(TOKENS, TOKENS)]


def group_lanes(half, i):
    return at_lanes(384 * (2 * half + i), 0, 384)


def inner_half(half, q_ref, kv_ref, accum_ref, inner_ref, start_ref, tail_ref):
    accum = half_rows(accum_ref, half)
    cols = columns(accum)
    start_ref[...] = jnp.exp(cols)
    tail_ref[...] = columns(jnp.exp(accum[:, LANES - 1 :] - accum))
    k_ref, v_ref = keys_of(kv_ref), values_of(kv_ref)
    for i in range(2):
        g = 2 * half + i
        tiles = [None] * 3
        for j in range(4):
            scores = dot_nt(head_tiles(q_ref, g, j, True), head_tiles(k_ref, g, j, False))
            weights = (scores * weight_of(accum, cols, 4 * i + j)).astype(BF16)
            add_tiles(tiles, dot_nn(weights, head_tiles(v_ref, g, j, True)), j)
        for t in range(3):
            inner_ref[:, 384 * i + LANES * t : 384 * i + LANES * t + LANES] = tiles[t]


def inner_kernel(
    core_ref, q_ref, kv_ref, accum_ref,
    own_inner_ref, own_start_ref, own_tail_ref, inner_ref, start_ref, tail_ref,
):
    core = core_ref[0]
    inner_half(core, q_ref, kv_ref, accum_ref, own_inner_ref, own_start_ref, own_tail_ref)
    inner_half(1 - core, q_ref, kv_ref, accum_ref, inner_ref, start_ref, tail_ref)


def attention_half(half, q_ref, y_ref, gain_ref, start_ref, inner_ref, state_ref, o_ref, squares, crossed):
    start = start_ref[...]
    for i in range(2):
        pairs = [pair_states(state_ref, i, p) for p in range(2)]
        lanes = group_lanes(half, i)
        at = slice(384 * i, 384 * i + 384)
        attention = inner_ref[:, at] + group_columns(start, i) * times_states(q_ref[:, lanes], pairs, dot_nn)
        o_ref[:, at] = attention
        both = gain_ref[:, lanes] * y_ref[:, lanes].astype(F32) * attention
        square = attention * attention
        for t in range(3):
            squares = squares + square[:, LANES * t : LANES * t + LANES]
            crossed = crossed + both[:, LANES * t : LANES * t + LANES]
    return squares, crossed


def attention_kernel(
    core_ref, q_ref, y_ref, gain_ref, own_start_ref, own_inner_ref, start_ref, inner_ref, own_ref, got_ref, got_x_ref,
    own_o_ref, other_o_ref, sums_ref, state_ref,
):
    core = core_ref[0]
    own_states(core, 1, own_ref, got_x_ref, got_x_ref, state_ref)
    zero = jnp.zeros((TOKENS, LANES), F32)
    squares, crossed = attention_half(
        core, q_ref, y_ref, gain_ref, own_start_ref, own_inner_ref, state_ref, own_o_ref, zero, zero
    )
    squares, crossed = attention_half(
        1 - core, q_ref, y_ref, gain_ref, start_ref, inner_ref, got_ref, other_o_ref, squares, crossed
    )
    sums_ref[0:1, :] = jnp.sum(squares.T, axis=0, keepdims=True)
    sums_ref[1:2, :] = jnp.sum(crossed.T, axis=0, keepdims=True)


def norm_kernel(
    core_ref, q_ref, y_ref, gain_ref, accum_ref, own_o_ref, other_o_ref, sums_0, sums_1, sums_2, sums_3, back_ref, c_ref
):
    sums = (sums_0[...] + sums_1[...]) + (sums_2[...] + sums_3[...])
    root = jnp.sqrt(sums[0:1, :] / (HEADS * HEAD_DIM) + 1e-05)
    factor = sums[1:2, :] / (HEADS * HEAD_DIM * root * root * root)
    cols = columns(jnp.concatenate([1.0 / root, factor], axis=0))
    inverse = jnp.broadcast_to(cols[:, 0:1], (TOKENS, 384))
    factor = jnp.broadcast_to(cols[:, 1:2], (TOKENS, 384))
    core = core_ref[0]
    for half, o_ref in ((1 - core, other_o_ref), (core, own_o_ref)):
        for i in range(2):
            lanes = group_lanes(half, i)
            scaled = gain_ref[:, lanes] * y_ref[:, lanes].astype(F32)
            back_ref[:, lanes] = (scaled * inverse - o_ref[:, 384 * i : 384 * i + 384] * factor).astype(BF16)
    half = 1 - core
    outer_states(half, q_ref, jnp.exp(half_rows(accum_ref, half)), back_ref, c_ref)


def carry_keep_kernel(core_ref, q_ref, back_ref, accum_ref, c_ref):
    half = core_ref[0]
    outer_states(half, q_ref, jnp.exp(half_rows(accum_ref, half)), back_ref, c_ref)


def middle_half(half, q_ref, kv_ref, back_ref, accum_ref, state_ref, gq_ref, gk_ref):
    accum = half_rows(accum_ref, half)
    cols = columns(accum)
    start = jnp.exp(cols)
    k_ref, v_ref = keys_of(kv_ref), values_of(kv_ref)
    for i in range(2):
        g = 2 * half + i
        pairs = [pair_states(state_ref, i, p) for p in range(2)]
        gq = group_columns(start, i) * times_states(back_ref[:, group_lanes(half, i)], pairs, dot_nt)
        gq = [gq[:, LANES * t : LANES * t + LANES] for t in range(3)]
        gk = [None] * 3
        for j in range(4):
            h = 4 * i + j
            q = head_tiles(q_ref, g, j, True)
            k = head_tiles(k_ref, g, j, True)
            v = head_tiles(v_ref, g, j, False)
            d = head_tiles(back_ref, g, j, True)
            weights = (dot_nt(d, v) * weight_of(accum, cols, h)).astype(BF16)
            weights_t = (dot_nt(v, d) * weight_turned(accum, cols, h)).astype(BF16)
            add_tiles(gq, dot_nn(weights, k), j)
            add_tiles(gk, dot_nn(weights_t, q), j)
        for t in range(3):
            gq_ref[:, at_lanes(384 * g, LANES * t, LANES)] = gq[t].astype(BF16)
            gk_ref[:, 384 * i + LANES * t : 384 * i + LANES * t + LANES] = gk[t]


def middle_kernel(
    core_ref, q_ref, kv_ref, back_ref, accum_ref, own_ref, got_x_ref, other_state_ref,
    gq_ref, own_gk_ref, other_gk_ref, done_ref, own_state_ref,
):
    done_ref[...] = accum_ref[0:8, :]
    core = core_ref[0]
    own_states(core, 1, own_ref, got_x_ref, got_x_ref, own_state_ref)
    middle_half(core, q_ref, kv_ref, back_ref, accum_ref, own_state_ref, gq_ref, own_gk_ref)
    middle_half(1 - core, q_ref, kv_ref, back_ref, accum_ref, other_state_ref, gq_ref, other_gk_ref)


def values_half(half, q_ref, kv_ref, back_ref, accum_ref, gv_ref):
    accum = half_rows(accum_ref, half)
    cols = columns(accum)
    k_ref = keys_of(kv_ref)
    for i in range(2):
        g = 2 * half + i
        gv = [None] * 3
        for j in range(4):
            scores = dot_nt(head_tiles(k_ref, g, j, True), head_tiles(q_ref, g, j, False))
            weights = (scores * weight_turned(accum, cols, 4 * i + j)).astype(BF16)
            add_tiles(gv, dot_nn(weights, head_tiles(back_ref, g, j, True)), j)
        for t in range(3):
            gv_ref[:, 384 * i + LANES * t : 384 * i + LANES * t + LANES] = gv[t]


def values_own_kernel(core_ref, q_ref, kv_ref, back_ref, accum_ref, gv_ref, done_ref):
    done_ref[...] = accum_ref[0:8, :]
    values_half(core_ref[0], q_ref, kv_ref, back_ref, accum_ref, gv_ref)


def values_other_kernel(core_ref, q_ref, kv_ref, back_ref, accum_ref, gv_ref):
    values_half(1 - core_ref[0], q_ref, kv_ref, back_ref, accum_ref, gv_ref)


def last_group(half, i, kv_ref, tail, gk0_ref, gv0_ref, carry_ref, gk_ref, gv_ref):
    pairs = [pair_states(carry_ref, i, p) for p in range(2)]
    lanes = group_lanes(half, i)
    at = slice(384 * i, 384 * i + 384)
    wide = group_columns(tail, i)
    k_ref, v_ref = keys_of(kv_ref), values_of(kv_ref)
    gk_ref[:, at] = (gk0_ref[:, at] + wide * times_states(v_ref[:, lanes], pairs, dot_nt)).astype(BF16)
    gv_ref[:, at] = (gv0_ref[:, at] + wide * times_states(k_ref[:, lanes], pairs, dot_nn)).astype(BF16)


def last_own_kernel(
    core_ref, kv_ref, tail_ref, gk0_ref, gv0_ref, own_ref, got_c_ref, got_x_ref, gk_ref, gv_ref, carry_ref
):
    core = core_ref[0]
    own_states(core, 0, own_ref, got_c_ref, got_x_ref, carry_ref)
    for i in range(2):
        last_group(core, i, kv_ref, tail_ref[...], gk0_ref, gv0_ref, carry_ref, gk_ref, gv_ref)


def last_other_kernel(
    core_ref, kv_ref, tail_ref, gk0_ref, gv0_ref, carry_ref, own_gk_ref, own_gv_ref,
    gk_hbm, gv_hbm, gk_ref, gv_ref, sems,
):
    core = core_ref[0]
    copies = []

    def copy_out(half, i, gk, gv, first):
        lanes = group_lanes(half, i)
        for n, (src, dst) in enumerate(((gk, gk_hbm), (gv, gv_hbm))):
            copy = pltpu.make_async_copy(src.at[:, pl.ds(384 * i, 384)], dst.at[:, lanes], sems.at[first + n])
            copy.start()
            copies.append(copy)

    for i in range(2):
        copy_out(core, i, own_gk_ref, own_gv_ref, 2 * i)
    for i in range(2):
        last_group(1 - core, i, kv_ref, tail_ref[...], gk0_ref, gv0_ref, carry_ref, gk_ref, gv_ref)
        copy_out(1 - core, i, gk_ref, gv_ref, 4 + 2 * i)
    for copy in copies:
        copy.wait()


def call(kernel, outs, smem, *args, hbm_in=(), hbm_out=(), scratch=(), flops=0):
    specs = []
    for i, arg in enumerate(args):
        space = pltpu.SMEM if i < smem else pltpu.HBM if i in hbm_in else pltpu.VMEM
        specs.append(pl.BlockSpec(memory_space=space))
    shapes = [jax.ShapeDtypeStruct(s, d) for s, d in outs]
    moved = sum(a.size * a.dtype.itemsize for a in args) + sum(s.size * s.dtype.itemsize for s in shapes)
    out = pl.pallas_call(
        kernel,
        out_shape=shapes,
        in_specs=specs,
        out_specs=[pl.BlockSpec(memory_space=pltpu.HBM if i in hbm_out else pltpu.VMEM) for i in range(len(shapes))],
        scratch_shapes=scratch,
        compiler_params=pltpu.CompilerParams(vmem_limit_bytes=VMEM),
        cost_estimate=pl.CostEstimate(flops=flops, bytes_accessed=moved, transcendentals=0),
        name=kernel.__name__,
    )(*args)
    return out[0] if len(out) == 1 else out


SWAP = [(0, 1), (1, 0)]
CHIP_BITS = ("xh", "xl", "zh", "zm", "zl")
EXCHANGE = ("zl", "zm", "xl", "xh", "zh")


def swap(value):
    return lax.ppermute(value, "core", SWAP)


def exchange(value):
    rows = value.shape[0] // CHIPS
    parts = value.reshape(CHIPS, rows // 2, 2, LANES) if rows % 2 == 0 else value.reshape(-1)
    return lax.all_to_all(parts, EXCHANGE, 0, 0, tiled=True).reshape(value.shape)


def others(value):
    return [lax.ppermute(value, "head", [(i, (i + k) % 4) for i in range(4)]) for k in (1, 2, 3)]


def local(q, k, v, y, logs, gain):
    core = lax.axis_index("core").astype(jnp.int32).reshape(1)
    gain = gain.reshape(1, WIDTH)
    half = ((HALF_ROWS, LANES), F32)
    half_decay = ((HALF_ROWS + HALF, LANES), F32)
    rows = ((LOCAL_HEADS, LANES), F32)
    cols = ((TOKENS, LANES), F32)
    token = ((8, LANES), F32)
    wide = (TOKENS, WIDTH)
    half_wide = ((TOKENS, WIDTH // 2), F32)
    narrow = pltpu.VMEM((TOKENS, WIDTH // 2), BF16)
    kv, logs = lax.optimization_barrier((jnp.concatenate([k, v]), logs))
    x_send, accum = call(state_send_kernel, [half_decay, rows], 1, core, kv, logs, flops=10**9)
    got_x = swap(x_send)
    x_keep = call(state_keep_kernel, [half_decay], 1, core, kv, accum, flops=10**9)
    payload = call(
        combine_forward_kernel, [((CHIPS * FWD_PART, LANES), F32)], 1, core, x_keep, got_x
    )
    payload = exchange(payload)
    entering, decays = call(scan_forward_kernel, [half, ((CHIPS, LANES), F32)], 0, payload)
    entering = exchange(entering)
    got_entering = swap(call(step_forward_kernel, [half], 1, core, entering, x_keep))
    own_inner, own_start, own_tail, inner, start, tail = call(
        inner_kernel, [half_wide, cols, cols, half_wide, cols, cols], 1, core, q, kv, accum, flops=2 * 10**9
    )
    half_scratch = pltpu.VMEM((HALF_ROWS, LANES), F32)
    own_o, other_o, sums = call(
        attention_kernel,
        [half_wide, half_wide, ((2, LANES), F32)],
        1, core, q, y, gain, own_start, own_inner, start, inner, entering, got_entering, got_x,
        scratch=[half_scratch],
        flops=10**9,
    )
    back, c_send = call(
        norm_kernel,
        [(wide, BF16), half],
        1, core, q, y, gain, accum, own_o, other_o, sums, *others(sums),
        flops=10**9,
    )
    got_c = swap(c_send)
    c_keep = call(carry_keep_kernel, [half], 1, core, q, back, accum, flops=5 * 10**8)
    own_gv, values_done = call(values_own_kernel, [half_wide, token], 1, core, q, kv, back, accum, flops=10**9)
    payload = call(combine_backward_kernel, [half], 1, core, c_keep, got_c, x_keep, got_x)
    payload = exchange(payload)
    gq, own_gk, other_gk, middle_done = call(
        middle_kernel,
        [(wide, BF16), half_wide, half_wide, token],
        1, core, q, kv, back, accum, entering, got_x, got_entering,
        scratch=[half_scratch],
        flops=4 * 10**9,
    )
    leaving = call(scan_backward_kernel, [half], 0, payload, decays, middle_done, values_done)
    leaving = exchange(leaving)
    got_leaving = swap(call(step_backward_kernel, [half], 1, core, leaving, c_keep, x_keep))
    other_gv = call(values_other_kernel, [half_wide], 1, core, q, kv, back, accum, flops=10**9)
    half_narrow = ((TOKENS, WIDTH // 2), BF16)
    own_gk, own_gv = call(
        last_own_kernel,
        [half_narrow, half_narrow],
        1, core, kv, own_tail, own_gk, own_gv, leaving, got_c, got_x,
        scratch=[half_scratch],
        flops=5 * 10**8,
    )
    gk, gv = call(
        last_other_kernel,
        [(wide, BF16), (wide, BF16)],
        1, core, kv, tail, other_gk, other_gv, got_leaving, own_gk, own_gv,
        hbm_out=(0, 1),
        scratch=[narrow, narrow, pltpu.SemaphoreType.DMA((8,))],
        flops=5 * 10**8,
    )
    return gq, gk, gv


def solution(mesh):
    tokens = (*CHIP_BITS, "core")
    grid = Mesh(mesh.devices.reshape(2, 2, 2, 2, 2, 2, 4), (*tokens, "head"))
    rows = P(tokens, "head")
    return jax.shard_map(
        local,
        mesh=grid,
        in_specs=(rows, rows, rows, rows, P("head", tokens), P("head")),
        out_specs=(rows, rows, rows),
        check_vma=False,
    )
```

```python
import jax
import jax.numpy as jnp
from jax import lax
from jax.experimental import pallas as pl
from jax.experimental.pallas import tpu as pltpu
from jax.sharding import Mesh, PartitionSpec as P

HEADS = 64
HEAD_DIM = 96
TOKENS = 128
LOCAL_HEADS = 16
HALF = 8
WIDTH = LOCAL_HEADS * HEAD_DIM
LANES = 128
PACK = 72
CHIPS = 32
PART = 18
FWD_PART = 19
ROWS = LOCAL_HEADS * PACK
HALF_ROWS = HALF * PACK
VMEM = 12 * 1024 * 1024

F32 = jnp.float32
BF16 = jnp.bfloat16

START = (0, 0, 128, 256)
SPAN = (128, 256, 256, 128)
FIRST = (0, 96, 64, 32)
FREE = (3, 2, 1, 0)


def lanes_of(shape):
    return lax.broadcasted_iota(jnp.int32, shape, len(shape) - 1)


def rows_of(shape):
    return lax.broadcasted_iota(jnp.int32, shape, len(shape) - 2)


def dot_nn(a, b):
    return lax.dot_general(a, b, (((1,), (0,)), ((), ())), preferred_element_type=F32)


def dot_nt(a, b):
    return lax.dot_general(a, b, (((1,), (1,)), ((), ())), preferred_element_type=F32)


def two(x):
    high = x.astype(BF16)
    return high, (x - high.astype(F32)).astype(BF16)


def at_lanes(base, start, size):
    return pl.ds(base + start if isinstance(base, int) else pl.multiple_of(base + start, LANES), size)


def head_tiles(value, g, j, masked):
    part = value[:, at_lanes(384 * g, START[j], SPAN[j])]
    if masked:
        lane = lanes_of(part.shape)
        part = jnp.where((lane >= FIRST[j]) & (lane < FIRST[j] + HEAD_DIM), part, jnp.zeros_like(part))
    return part


def merge(tiles):
    return tiles if tiles.shape[1] == LANES else tiles[:, :LANES] + tiles[:, LANES:]


def pack(square, j):
    lane = lanes_of((24, LANES))
    free = lane // 32 == FREE[j]
    extra = square[PACK:]
    others = [c for c in range(4) if c != FREE[j]]
    return [
        jnp.where(free, pltpu.roll(extra, (32 * (FREE[j] - c)) % LANES, 1), square[24 * i : 24 * i + 24])
        for i, c in enumerate(others)
    ]


def unpack(packed, j):
    lane = lanes_of((24, LANES))
    others = [c for c in range(4) if c != FREE[j]]
    extra = jnp.zeros((24, LANES), F32)
    for i, c in enumerate(others):
        moved = pltpu.roll(packed[24 * i : 24 * i + 24], (32 * (c - FREE[j])) % LANES, 1)
        extra = jnp.where(lane // 32 == c, moved, extra)
    return jnp.concatenate([packed, extra], axis=0)


def spread(square, j):
    lane = lanes_of(square.shape)
    zero = jnp.zeros_like(square)
    if j == 0:
        tiles = (jnp.where(lane < 96, square, zero), zero)
    elif j == 1:
        tiles = (jnp.where(lane >= 96, square, zero), jnp.where(lane < 64, square, zero))
    elif j == 2:
        tiles = (jnp.where(lane >= 64, square, zero), jnp.where(lane < 32, square, zero))
    else:
        tiles = (zero, jnp.where(lane >= 32, square, zero))
    return jnp.concatenate(tiles, axis=1)


def pair_states(ref, g, pair):
    parts = []
    for j in (2 * pair, 2 * pair + 1):
        h = 4 * g + j
        parts.append([spread(part, j) for part in two(unpack(ref[PACK * h : PACK * h + PACK, :], j))])
    zero = jnp.zeros((64, 256), BF16)
    out = []
    for first, second in zip(*parts):
        rows = [first, second, zero] if pair == 0 else [zero, first, second]
        out.append(jnp.concatenate(rows, axis=0))
    return out


def times_states(values, pairs, dot):
    left, right = (
        dot(values[:, LANES * p : LANES * p + 256], pairs[p][0])
        + dot(values[:, LANES * p : LANES * p + 256], pairs[p][1])
        for p in range(2)
    )
    return jnp.concatenate([left[:, :LANES], left[:, LANES:] + right[:, :LANES], right[:, LANES:]], axis=1)


def running(logs):
    high = logs.astype(BF16)
    rest = logs - high.astype(F32)
    middle = rest.astype(BF16)
    low = (rest - middle.astype(F32)).astype(BF16)
    shape = (LANES, LANES)
    upto = jnp.where(rows_of(shape) <= lanes_of(shape), 1.0, 0.0).astype(BF16)
    return dot_nn(low, upto) + dot_nn(middle, upto) + dot_nn(high, upto)


def columns(rows):
    filler = jnp.zeros((LANES - rows.shape[0], LANES), F32)
    return jnp.concatenate([rows, filler], axis=0).T


def wide_column(cols, h):
    return jnp.broadcast_to(cols[:, h : h + 1], (TOKENS, LANES))


def group_columns(cols, g):
    lane = lanes_of((TOKENS, LANES))
    c = [wide_column(cols, 4 * g + j) for j in range(4)]
    return jnp.concatenate(
        [jnp.where(lane < 96, c[0], c[1]), jnp.where(lane < 64, c[1], c[2]), jnp.where(lane < 32, c[2], c[3])],
        axis=1,
    )


def weight_of(accum, cols, h):
    row = accum[h : h + 1, :]
    spread_by = wide_column(cols, h) - row
    shape = (TOKENS, LANES)
    keep = lanes_of(shape) <= rows_of(shape)
    return jnp.exp(jnp.where(keep, spread_by, -jnp.inf))


def weight_turned(accum, cols, h):
    spread_by = accum[h : h + 1, :] - wide_column(cols, h)
    shape = (TOKENS, LANES)
    keep = rows_of(shape) <= lanes_of(shape)
    return jnp.exp(jnp.where(keep, spread_by, -jnp.inf))


def outer_states(half, left_ref, scale, right_ref, out_ref):
    for i in range(2):
        g = 2 * half + i
        turned = left_ref[:, at_lanes(384 * g, 0, 384)].astype(F32).T
        for j in range(4):
            h = 4 * i + j
            left = jnp.concatenate(two(turned[96 * j : 96 * j + 96, :] * scale[h : h + 1, :]), axis=0)
            both = dot_nn(left, head_tiles(right_ref, g, j, True))
            square = merge(both[:96] + both[96:])
            for n, piece in enumerate(pack(square, j)):
                out_ref[PACK * h + 24 * n : PACK * h + 24 * n + 24, :] = piece


def half_rows(ref, half):
    return ref[pl.ds(pl.multiple_of(HALF * half, HALF), HALF), :]


def state_half(half, kv_ref, accum_ref, out_ref):
    accum = half_rows(accum_ref, half)
    last = jnp.broadcast_to(accum[:, LANES - 1 :], (HALF, LANES))
    out_ref[HALF_ROWS : HALF_ROWS + HALF, :] = jnp.exp(last)
    keys, values = kv_ref.at[pl.ds(0, TOKENS)], kv_ref.at[pl.ds(TOKENS, TOKENS)]
    outer_states(half, keys, jnp.exp(last - accum), values, out_ref)


def state_send_kernel(core_ref, kv_ref, logs_ref, out_ref, accum_ref):
    accum_ref[...] = running(logs_ref[...])
    state_half(1 - core_ref[0], kv_ref, accum_ref, out_ref)


def state_keep_kernel(core_ref, kv_ref, accum_ref, out_ref):
    state_half(core_ref[0], kv_ref, accum_ref, out_ref)


def combine_forward_kernel(core_ref, own_ref, got_ref, out_ref):
    first = core_ref[0] == 0
    own_decay = own_ref[HALF_ROWS : HALF_ROWS + HALF, :]
    got_decay = got_ref[HALF_ROWS : HALF_ROWS + HALF, :]
    late_decay = jnp.where(first, got_decay, own_decay)
    both_decay = own_decay * got_decay
    for h in range(HALF):
        own = own_ref[PACK * h : PACK * h + PACK, :]
        got = got_ref[PACK * h : PACK * h + PACK, :]
        early = jnp.where(first, own, got)
        late = jnp.where(first, got, own)
        total = early * late_decay[h : h + 1, :] + late
        for quarter in range(4):
            to = FWD_PART * (4 * h + quarter)
            out_ref[to : to + PART, :] = total[PART * quarter : PART * quarter + PART, :]
            out_ref[to + PART : to + FWD_PART, :] = both_decay[h : h + 1, :]


def combine_backward_kernel(core_ref, own_ref, got_ref, own_x_ref, got_x_ref, out_ref):
    first = core_ref[0] == 0
    at = slice(HALF_ROWS, HALF_ROWS + HALF)
    early_decay = jnp.where(first, own_x_ref[at, :], got_x_ref[at, :])
    for h in range(HALF):
        own = own_ref[PACK * h : PACK * h + PACK, :]
        got = got_ref[PACK * h : PACK * h + PACK, :]
        early = jnp.where(first, own, got)
        late = jnp.where(first, got, own)
        out_ref[PACK * h : PACK * h + PACK, :] = late * early_decay[h : h + 1, :] + early


def place_of(c):
    return sum(((c >> (4 - CHIP_BITS.index(name))) & 1) << (4 - i) for i, name in enumerate(EXCHANGE))


def scan_forward_kernel(in_ref, out_ref, decay_ref):
    state = jnp.zeros((PART, LANES), F32)
    for c in range(CHIPS):
        place = place_of(c)
        out_ref[PART * place : PART * place + PART, :] = state
        at = FWD_PART * place
        decay = in_ref[at + PART : at + PART + 1, :]
        decay_ref[c : c + 1, :] = decay
        state = state * decay + in_ref[at : at + PART, :]


def scan_backward_kernel(in_ref, decay_ref, after_ref, after_too_ref, out_ref):
    state = jnp.zeros((PART, LANES), F32)
    for c in reversed(range(CHIPS)):
        at = PART * place_of(c)
        out_ref[at : at + PART, :] = state
        state = state * decay_ref[c : c + 1, :] + in_ref[at : at + PART, :]


def step_kernel(core_ref, stepping, state_ref, add_ref, decay_ref, out_ref):
    steps = core_ref[0] == stepping
    for h in range(HALF):
        at = slice(PACK * h, PACK * h + PACK)
        state = state_ref[at, :]
        stepped = state * decay_ref[HALF_ROWS + h : HALF_ROWS + h + 1, :] + add_ref[at, :]
        out_ref[at, :] = jnp.where(steps, stepped, state)


def step_forward_kernel(core_ref, state_ref, x_ref, out_ref):
    step_kernel(core_ref, 0, state_ref, x_ref, x_ref, out_ref)


def step_backward_kernel(core_ref, state_ref, c_ref, x_ref, out_ref):
    step_kernel(core_ref, 1, state_ref, c_ref, x_ref, out_ref)


def own_states(core, late, own_ref, add_ref, decay_ref, out_ref):
    for h in range(HALF):
        at = slice(PACK * h, PACK * h + PACK)
        own = own_ref[at, :]
        stepped = own * decay_ref[HALF_ROWS + h : HALF_ROWS + h + 1, :] + add_ref[at, :]
        out_ref[at, :] = jnp.where(core == late, stepped, own)


def add_tiles(tiles, part, j):
    for i in range(SPAN[j] // LANES):
        t = START[j] // LANES + i
        piece = part[:, LANES * i : LANES * i + LANES]
        tiles[t] = piece if tiles[t] is None else tiles[t] + piece


def keys_of(kv_ref):
    return kv_ref.at[pl.ds(0, TOKENS)]


def values_of(kv_ref):
    return kv_ref.at[pl.ds(TOKENS, TOKENS)]


def group_lanes(half, i):
    return at_lanes(384 * (2 * half + i), 0, 384)


def inner_half(half, q_ref, kv_ref, accum_ref, inner_ref, start_ref, tail_ref):
    accum = half_rows(accum_ref, half)
    cols = columns(accum)
    start_ref[...] = jnp.exp(cols)
    tail_ref[...] = columns(jnp.exp(accum[:, LANES - 1 :] - accum))
    k_ref, v_ref = keys_of(kv_ref), values_of(kv_ref)
    for i in range(2):
        g = 2 * half + i
        tiles = [None] * 3
        for j in range(4):
            scores = dot_nt(head_tiles(q_ref, g, j, True), head_tiles(k_ref, g, j, False))
            weights = (scores * weight_of(accum, cols, 4 * i + j)).astype(BF16)
            add_tiles(tiles, dot_nn(weights, head_tiles(v_ref, g, j, True)), j)
        for t in range(3):
            inner_ref[:, 384 * i + LANES * t : 384 * i + LANES * t + LANES] = tiles[t]


def inner_kernel(
    core_ref, q_ref, kv_ref, accum_ref,
    own_inner_ref, own_start_ref, own_tail_ref, inner_ref, start_ref, tail_ref,
):
    core = core_ref[0]
    inner_half(core, q_ref, kv_ref, accum_ref, own_inner_ref, own_start_ref, own_tail_ref)
    inner_half(1 - core, q_ref, kv_ref, accum_ref, inner_ref, start_ref, tail_ref)


def attention_half(half, q_ref, y_ref, gain_ref, start_ref, inner_ref, state_ref, o_ref, squares, crossed):
    start = start_ref[...]
    for i in range(2):
        pairs = [pair_states(state_ref, i, p) for p in range(2)]
        lanes = group_lanes(half, i)
        at = slice(384 * i, 384 * i + 384)
        attention = inner_ref[:, at] + group_columns(start, i) * times_states(q_ref[:, lanes], pairs, dot_nn)
        o_ref[:, at] = attention
        both = gain_ref[:, lanes] * y_ref[:, lanes].astype(F32) * attention
        square = attention * attention
        for t in range(3):
            squares = squares + square[:, LANES * t : LANES * t + LANES]
            crossed = crossed + both[:, LANES * t : LANES * t + LANES]
    return squares, crossed


def attention_kernel(
    core_ref, q_ref, y_ref, gain_ref, own_start_ref, own_inner_ref, start_ref, inner_ref, own_ref, got_ref, got_x_ref,
    own_o_ref, other_o_ref, sums_ref, state_ref,
):
    core = core_ref[0]
    own_states(core, 1, own_ref, got_x_ref, got_x_ref, state_ref)
    zero = jnp.zeros((TOKENS, LANES), F32)
    squares, crossed = attention_half(
        core, q_ref, y_ref, gain_ref, own_start_ref, own_inner_ref, state_ref, own_o_ref, zero, zero
    )
    squares, crossed = attention_half(
        1 - core, q_ref, y_ref, gain_ref, start_ref, inner_ref, got_ref, other_o_ref, squares, crossed
    )
    sums_ref[0:1, :] = jnp.sum(squares.T, axis=0, keepdims=True)
    sums_ref[1:2, :] = jnp.sum(crossed.T, axis=0, keepdims=True)


def norm_kernel(
    core_ref, q_ref, y_ref, gain_ref, accum_ref, own_o_ref, other_o_ref, sums_0, sums_1, sums_2, sums_3, back_ref, c_ref
):
    sums = (sums_0[...] + sums_1[...]) + (sums_2[...] + sums_3[...])
    root = jnp.sqrt(sums[0:1, :] / (HEADS * HEAD_DIM) + 1e-05)
    factor = sums[1:2, :] / (HEADS * HEAD_DIM * root * root * root)
    cols = columns(jnp.concatenate([1.0 / root, factor], axis=0))
    inverse = jnp.broadcast_to(cols[:, 0:1], (TOKENS, 384))
    factor = jnp.broadcast_to(cols[:, 1:2], (TOKENS, 384))
    core = core_ref[0]
    for half, o_ref in ((1 - core, other_o_ref), (core, own_o_ref)):
        for i in range(2):
            lanes = group_lanes(half, i)
            scaled = gain_ref[:, lanes] * y_ref[:, lanes].astype(F32)
            back_ref[:, lanes] = (scaled * inverse - o_ref[:, 384 * i : 384 * i + 384] * factor).astype(BF16)
    half = 1 - core
    outer_states(half, q_ref, jnp.exp(half_rows(accum_ref, half)), back_ref, c_ref)


def carry_keep_kernel(core_ref, q_ref, back_ref, accum_ref, c_ref):
    half = core_ref[0]
    outer_states(half, q_ref, jnp.exp(half_rows(accum_ref, half)), back_ref, c_ref)


def middle_half(half, q_ref, kv_ref, back_ref, accum_ref, state_ref, gq_ref, gk_ref):
    accum = half_rows(accum_ref, half)
    cols = columns(accum)
    start = jnp.exp(cols)
    k_ref, v_ref = keys_of(kv_ref), values_of(kv_ref)
    for i in range(2):
        g = 2 * half + i
        pairs = [pair_states(state_ref, i, p) for p in range(2)]
        gq = group_columns(start, i) * times_states(back_ref[:, group_lanes(half, i)], pairs, dot_nt)
        gq = [gq[:, LANES * t : LANES * t + LANES] for t in range(3)]
        gk = [None] * 3
        for j in range(4):
            h = 4 * i + j
            q = head_tiles(q_ref, g, j, True)
            k = head_tiles(k_ref, g, j, True)
            v = head_tiles(v_ref, g, j, False)
            d = head_tiles(back_ref, g, j, True)
            weights = (dot_nt(d, v) * weight_of(accum, cols, h)).astype(BF16)
            weights_t = (dot_nt(v, d) * weight_turned(accum, cols, h)).astype(BF16)
            add_tiles(gq, dot_nn(weights, k), j)
            add_tiles(gk, dot_nn(weights_t, q), j)
        for t in range(3):
            gq_ref[:, at_lanes(384 * g, LANES * t, LANES)] = gq[t].astype(BF16)
            gk_ref[:, 384 * i + LANES * t : 384 * i + LANES * t + LANES] = gk[t]


def middle_kernel(
    core_ref, q_ref, kv_ref, back_ref, accum_ref, own_ref, got_x_ref, other_state_ref,
    gq_ref, own_gk_ref, other_gk_ref, done_ref, own_state_ref,
):
    done_ref[...] = accum_ref[0:8, :]
    core = core_ref[0]
    own_states(core, 1, own_ref, got_x_ref, got_x_ref, own_state_ref)
    middle_half(core, q_ref, kv_ref, back_ref, accum_ref, own_state_ref, gq_ref, own_gk_ref)
    middle_half(1 - core, q_ref, kv_ref, back_ref, accum_ref, other_state_ref, gq_ref, other_gk_ref)


def values_half(half, q_ref, kv_ref, back_ref, accum_ref, gv_ref):
    accum = half_rows(accum_ref, half)
    cols = columns(accum)
    k_ref = keys_of(kv_ref)
    for i in range(2):
        g = 2 * half + i
        gv = [None] * 3
        for j in range(4):
            scores = dot_nt(head_tiles(k_ref, g, j, True), head_tiles(q_ref, g, j, False))
            weights = (scores * weight_turned(accum, cols, 4 * i + j)).astype(BF16)
            add_tiles(gv, dot_nn(weights, head_tiles(back_ref, g, j, True)), j)
        for t in range(3):
            gv_ref[:, 384 * i + LANES * t : 384 * i + LANES * t + LANES] = gv[t]


def values_own_kernel(core_ref, q_ref, kv_ref, back_ref, accum_ref, gv_ref, done_ref):
    done_ref[...] = accum_ref[0:8, :]
    values_half(core_ref[0], q_ref, kv_ref, back_ref, accum_ref, gv_ref)


def values_other_kernel(core_ref, q_ref, kv_ref, back_ref, accum_ref, gv_ref):
    values_half(1 - core_ref[0], q_ref, kv_ref, back_ref, accum_ref, gv_ref)


def last_group(half, i, kv_ref, tail, gk0_ref, gv0_ref, carry_ref, gk_ref, gv_ref):
    pairs = [pair_states(carry_ref, i, p) for p in range(2)]
    lanes = group_lanes(half, i)
    at = slice(384 * i, 384 * i + 384)
    wide = group_columns(tail, i)
    k_ref, v_ref = keys_of(kv_ref), values_of(kv_ref)
    gk_ref[:, at] = (gk0_ref[:, at] + wide * times_states(v_ref[:, lanes], pairs, dot_nt)).astype(BF16)
    gv_ref[:, at] = (gv0_ref[:, at] + wide * times_states(k_ref[:, lanes], pairs, dot_nn)).astype(BF16)


def last_own_kernel(
    core_ref, kv_ref, tail_ref, gk0_ref, gv0_ref, own_ref, got_c_ref, got_x_ref, gk_ref, gv_ref, carry_ref
):
    core = core_ref[0]
    own_states(core, 0, own_ref, got_c_ref, got_x_ref, carry_ref)
    for i in range(2):
        last_group(core, i, kv_ref, tail_ref[...], gk0_ref, gv0_ref, carry_ref, gk_ref, gv_ref)


def last_other_kernel(
    core_ref, kv_ref, tail_ref, gk0_ref, gv0_ref, carry_ref, own_gk_ref, own_gv_ref,
    gk_hbm, gv_hbm, gk_ref, gv_ref, sems,
):
    core = core_ref[0]
    copies = []

    def copy_out(half, i, gk, gv, first):
        lanes = group_lanes(half, i)
        for n, (src, dst) in enumerate(((gk, gk_hbm), (gv, gv_hbm))):
            copy = pltpu.make_async_copy(src.at[:, pl.ds(384 * i, 384)], dst.at[:, lanes], sems.at[first + n])
            copy.start()
            copies.append(copy)

    for i in range(2):
        copy_out(core, i, own_gk_ref, own_gv_ref, 2 * i)
    for i in range(2):
        last_group(1 - core, i, kv_ref, tail_ref[...], gk0_ref, gv0_ref, carry_ref, gk_ref, gv_ref)
        copy_out(1 - core, i, gk_ref, gv_ref, 4 + 2 * i)
    for copy in copies:
        copy.wait()


def call(kernel, outs, smem, *args, hbm_in=(), hbm_out=(), scratch=(), flops=0):
    specs = []
    for i, arg in enumerate(args):
        space = pltpu.SMEM if i < smem else pltpu.HBM if i in hbm_in else pltpu.VMEM
        specs.append(pl.BlockSpec(memory_space=space))
    shapes = [jax.ShapeDtypeStruct(s, d) for s, d in outs]
    moved = sum(a.size * a.dtype.itemsize for a in args) + sum(s.size * s.dtype.itemsize for s in shapes)
    out = pl.pallas_call(
        kernel,
        out_shape=shapes,
        in_specs=specs,
        out_specs=[pl.BlockSpec(memory_space=pltpu.HBM if i in hbm_out else pltpu.VMEM) for i in range(len(shapes))],
        scratch_shapes=scratch,
        compiler_params=pltpu.CompilerParams(vmem_limit_bytes=VMEM),
        cost_estimate=pl.CostEstimate(flops=flops, bytes_accessed=moved, transcendentals=0),
        name=kernel.__name__,
    )(*args)
    return out[0] if len(out) == 1 else out


SWAP = [(0, 1), (1, 0)]
CHIP_BITS = ("xh", "xl", "zh", "zm", "zl")
EXCHANGE = ("zm", "zh", "xh", "zl", "xl")


def swap(value):
    return lax.ppermute(value, "core", SWAP)


def exchange(value):
    rows = value.shape[0] // CHIPS
    parts = value.reshape(CHIPS, rows // 2, 2, LANES) if rows % 2 == 0 else value.reshape(-1)
    return lax.all_to_all(parts, EXCHANGE, 0, 0, tiled=True).reshape(value.shape)


def others(value):
    return [lax.ppermute(value, "head", [(i, (i + k) % 4) for i in range(4)]) for k in (1, 2, 3)]


def local(q, k, v, y, logs, gain):
    core = lax.axis_index("core").astype(jnp.int32).reshape(1)
    gain = gain.reshape(1, WIDTH)
    half = ((HALF_ROWS, LANES), F32)
    half_decay = ((HALF_ROWS + HALF, LANES), F32)
    rows = ((LOCAL_HEADS, LANES), F32)
    cols = ((TOKENS, LANES), F32)
    token = ((8, LANES), F32)
    wide = (TOKENS, WIDTH)
    half_wide = ((TOKENS, WIDTH // 2), F32)
    narrow = pltpu.VMEM((TOKENS, WIDTH // 2), BF16)
    kv, logs = lax.optimization_barrier((jnp.concatenate([k, v]), logs))
    x_send, accum = call(state_send_kernel, [half_decay, rows], 1, core, kv, logs, flops=10**9)
    got_x = swap(x_send)
    x_keep = call(state_keep_kernel, [half_decay], 1, core, kv, accum, flops=10**9)
    payload = call(
        combine_forward_kernel, [((CHIPS * FWD_PART, LANES), F32)], 1, core, x_keep, got_x
    )
    payload = exchange(payload)
    entering, decays = call(scan_forward_kernel, [half, ((CHIPS, LANES), F32)], 0, payload)
    entering = exchange(entering)
    got_entering = swap(call(step_forward_kernel, [half], 1, core, entering, x_keep))
    own_inner, own_start, own_tail, inner, start, tail = call(
        inner_kernel, [half_wide, cols, cols, half_wide, cols, cols], 1, core, q, kv, accum, flops=2 * 10**9
    )
    half_scratch = pltpu.VMEM((HALF_ROWS, LANES), F32)
    own_o, other_o, sums = call(
        attention_kernel,
        [half_wide, half_wide, ((2, LANES), F32)],
        1, core, q, y, gain, own_start, own_inner, start, inner, entering, got_entering, got_x,
        scratch=[half_scratch],
        flops=10**9,
    )
    back, c_send = call(
        norm_kernel,
        [(wide, BF16), half],
        1, core, q, y, gain, accum, own_o, other_o, sums, *others(sums),
        flops=10**9,
    )
    got_c = swap(c_send)
    c_keep = call(carry_keep_kernel, [half], 1, core, q, back, accum, flops=5 * 10**8)
    own_gv, values_done = call(values_own_kernel, [half_wide, token], 1, core, q, kv, back, accum, flops=10**9)
    payload = call(combine_backward_kernel, [half], 1, core, c_keep, got_c, x_keep, got_x)
    payload = exchange(payload)
    gq, own_gk, other_gk, middle_done = call(
        middle_kernel,
        [(wide, BF16), half_wide, half_wide, token],
        1, core, q, kv, back, accum, entering, got_x, got_entering,
        scratch=[half_scratch],
        flops=4 * 10**9,
    )
    leaving = call(scan_backward_kernel, [half], 0, payload, decays, middle_done, values_done)
    leaving = exchange(leaving)
    got_leaving = swap(call(step_backward_kernel, [half], 1, core, leaving, c_keep, x_keep))
    other_gv = call(values_other_kernel, [half_wide], 1, core, q, kv, back, accum, flops=10**9)
    half_narrow = ((TOKENS, WIDTH // 2), BF16)
    own_gk, own_gv = call(
        last_own_kernel,
        [half_narrow, half_narrow],
        1, core, kv, own_tail, own_gk, own_gv, leaving, got_c, got_x,
        scratch=[half_scratch],
        flops=5 * 10**8,
    )
    gk, gv = call(
        last_other_kernel,
        [(wide, BF16), (wide, BF16)],
        1, core, kv, tail, other_gk, other_gv, got_leaving, own_gk, own_gv,
        hbm_out=(0, 1),
        scratch=[narrow, narrow, pltpu.SemaphoreType.DMA((8,))],
        flops=5 * 10**8,
    )
    return gq, gk, gv


def solution(mesh):
    tokens = (*CHIP_BITS, "core")
    grid = Mesh(mesh.devices.reshape(2, 2, 2, 2, 2, 2, 4), (*tokens, "head"))
    rows = P(tokens, "head")
    return jax.shard_map(
        local,
        mesh=grid,
        in_specs=(rows, rows, rows, rows, P("head", tokens), P("head")),
        out_specs=(rows, rows, rows),
        check_vma=False,
    )
```

```python
import jax
import jax.numpy as jnp
from jax import lax
from jax.experimental import pallas as pl
from jax.experimental.pallas import tpu as pltpu
from jax.sharding import Mesh, PartitionSpec as P

HEADS = 64
HEAD_DIM = 96
TOKENS = 128
LOCAL_HEADS = 16
HALF = 8
WIDTH = LOCAL_HEADS * HEAD_DIM
LANES = 128
PACK = 72
CHIPS = 32
PART = 18
FWD_PART = 19
ROWS = LOCAL_HEADS * PACK
HALF_ROWS = HALF * PACK
VMEM = 12 * 1024 * 1024

F32 = jnp.float32
BF16 = jnp.bfloat16

START = (0, 0, 128, 256)
SPAN = (128, 256, 256, 128)
FIRST = (0, 96, 64, 32)
FREE = (3, 2, 1, 0)


def lanes_of(shape):
    return lax.broadcasted_iota(jnp.int32, shape, len(shape) - 1)


def rows_of(shape):
    return lax.broadcasted_iota(jnp.int32, shape, len(shape) - 2)


def dot_nn(a, b):
    return lax.dot_general(a, b, (((1,), (0,)), ((), ())), preferred_element_type=F32)


def dot_nt(a, b):
    return lax.dot_general(a, b, (((1,), (1,)), ((), ())), preferred_element_type=F32)


def two(x):
    high = x.astype(BF16)
    return high, (x - high.astype(F32)).astype(BF16)


def at_lanes(base, start, size):
    return pl.ds(base + start if isinstance(base, int) else pl.multiple_of(base + start, LANES), size)


def head_tiles(value, g, j, masked):
    part = value[:, at_lanes(384 * g, START[j], SPAN[j])]
    if masked:
        lane = lanes_of(part.shape)
        part = jnp.where((lane >= FIRST[j]) & (lane < FIRST[j] + HEAD_DIM), part, jnp.zeros_like(part))
    return part


def merge(tiles):
    return tiles if tiles.shape[1] == LANES else tiles[:, :LANES] + tiles[:, LANES:]


def pack(square, j):
    lane = lanes_of((24, LANES))
    free = lane // 32 == FREE[j]
    extra = square[PACK:]
    others = [c for c in range(4) if c != FREE[j]]
    return [
        jnp.where(free, pltpu.roll(extra, (32 * (FREE[j] - c)) % LANES, 1), square[24 * i : 24 * i + 24])
        for i, c in enumerate(others)
    ]


def unpack(packed, j):
    lane = lanes_of((24, LANES))
    others = [c for c in range(4) if c != FREE[j]]
    extra = jnp.zeros((24, LANES), F32)
    for i, c in enumerate(others):
        moved = pltpu.roll(packed[24 * i : 24 * i + 24], (32 * (c - FREE[j])) % LANES, 1)
        extra = jnp.where(lane // 32 == c, moved, extra)
    return jnp.concatenate([packed, extra], axis=0)


def spread(square, j):
    lane = lanes_of(square.shape)
    zero = jnp.zeros_like(square)
    if j == 0:
        tiles = (jnp.where(lane < 96, square, zero), zero)
    elif j == 1:
        tiles = (jnp.where(lane >= 96, square, zero), jnp.where(lane < 64, square, zero))
    elif j == 2:
        tiles = (jnp.where(lane >= 64, square, zero), jnp.where(lane < 32, square, zero))
    else:
        tiles = (zero, jnp.where(lane >= 32, square, zero))
    return jnp.concatenate(tiles, axis=1)


def pair_states(ref, g, pair):
    parts = []
    for j in (2 * pair, 2 * pair + 1):
        h = 4 * g + j
        parts.append([spread(part, j) for part in two(unpack(ref[PACK * h : PACK * h + PACK, :], j))])
    zero = jnp.zeros((64, 256), BF16)
    out = []
    for first, second in zip(*parts):
        rows = [first, second, zero] if pair == 0 else [zero, first, second]
        out.append(jnp.concatenate(rows, axis=0))
    return out


def times_states(values, pairs, dot):
    left, right = (
        dot(values[:, LANES * p : LANES * p + 256], pairs[p][0])
        + dot(values[:, LANES * p : LANES * p + 256], pairs[p][1])
        for p in range(2)
    )
    return jnp.concatenate([left[:, :LANES], left[:, LANES:] + right[:, :LANES], right[:, LANES:]], axis=1)


def running(logs):
    high = logs.astype(BF16)
    rest = logs - high.astype(F32)
    middle = rest.astype(BF16)
    low = (rest - middle.astype(F32)).astype(BF16)
    shape = (LANES, LANES)
    upto = jnp.where(rows_of(shape) <= lanes_of(shape), 1.0, 0.0).astype(BF16)
    return dot_nn(low, upto) + dot_nn(middle, upto) + dot_nn(high, upto)


def columns(rows):
    filler = jnp.zeros((LANES - rows.shape[0], LANES), F32)
    return jnp.concatenate([rows, filler], axis=0).T


def wide_column(cols, h):
    return jnp.broadcast_to(cols[:, h : h + 1], (TOKENS, LANES))


def group_columns(cols, g):
    lane = lanes_of((TOKENS, LANES))
    c = [wide_column(cols, 4 * g + j) for j in range(4)]
    return jnp.concatenate(
        [jnp.where(lane < 96, c[0], c[1]), jnp.where(lane < 64, c[1], c[2]), jnp.where(lane < 32, c[2], c[3])],
        axis=1,
    )


def weight_of(accum, cols, h):
    row = accum[h : h + 1, :]
    spread_by = wide_column(cols, h) - row
    shape = (TOKENS, LANES)
    keep = lanes_of(shape) <= rows_of(shape)
    return jnp.exp(jnp.where(keep, spread_by, -jnp.inf))


def weight_turned(accum, cols, h):
    spread_by = accum[h : h + 1, :] - wide_column(cols, h)
    shape = (TOKENS, LANES)
    keep = rows_of(shape) <= lanes_of(shape)
    return jnp.exp(jnp.where(keep, spread_by, -jnp.inf))


def outer_states(half, left_ref, scale, right_ref, out_ref):
    for i in range(2):
        g = 2 * half + i
        turned = left_ref[:, at_lanes(384 * g, 0, 384)].astype(F32).T
        for j in range(4):
            h = 4 * i + j
            left = jnp.concatenate(two(turned[96 * j : 96 * j + 96, :] * scale[h : h + 1, :]), axis=0)
            both = dot_nn(left, head_tiles(right_ref, g, j, True))
            square = merge(both[:96] + both[96:])
            for n, piece in enumerate(pack(square, j)):
                out_ref[PACK * h + 24 * n : PACK * h + 24 * n + 24, :] = piece


def half_rows(ref, half):
    return ref[pl.ds(pl.multiple_of(HALF * half, HALF), HALF), :]


def state_half(half, kv_ref, accum_ref, out_ref):
    accum = half_rows(accum_ref, half)
    last = jnp.broadcast_to(accum[:, LANES - 1 :], (HALF, LANES))
    out_ref[HALF_ROWS : HALF_ROWS + HALF, :] = jnp.exp(last)
    keys, values = kv_ref.at[pl.ds(0, TOKENS)], kv_ref.at[pl.ds(TOKENS, TOKENS)]
    outer_states(half, keys, jnp.exp(last - accum), values, out_ref)


def state_send_kernel(core_ref, kv_ref, logs_ref, out_ref, accum_ref):
    accum_ref[...] = running(logs_ref[...])
    state_half(1 - core_ref[0], kv_ref, accum_ref, out_ref)


def state_keep_kernel(core_ref, kv_ref, accum_ref, out_ref):
    state_half(core_ref[0], kv_ref, accum_ref, out_ref)


def combine_forward_kernel(core_ref, own_ref, got_ref, out_ref):
    first = core_ref[0] == 0
    own_decay = own_ref[HALF_ROWS : HALF_ROWS + HALF, :]
    got_decay = got_ref[HALF_ROWS : HALF_ROWS + HALF, :]
    late_decay = jnp.where(first, got_decay, own_decay)
    both_decay = own_decay * got_decay
    for h in range(HALF):
        own = own_ref[PACK * h : PACK * h + PACK, :]
        got = got_ref[PACK * h : PACK * h + PACK, :]
        early = jnp.where(first, own, got)
        late = jnp.where(first, got, own)
        total = early * late_decay[h : h + 1, :] + late
        for quarter in range(4):
            to = FWD_PART * (4 * h + quarter)
            out_ref[to : to + PART, :] = total[PART * quarter : PART * quarter + PART, :]
            out_ref[to + PART : to + FWD_PART, :] = both_decay[h : h + 1, :]


def combine_backward_kernel(core_ref, own_ref, got_ref, own_x_ref, got_x_ref, out_ref):
    first = core_ref[0] == 0
    at = slice(HALF_ROWS, HALF_ROWS + HALF)
    early_decay = jnp.where(first, own_x_ref[at, :], got_x_ref[at, :])
    for h in range(HALF):
        own = own_ref[PACK * h : PACK * h + PACK, :]
        got = got_ref[PACK * h : PACK * h + PACK, :]
        early = jnp.where(first, own, got)
        late = jnp.where(first, got, own)
        out_ref[PACK * h : PACK * h + PACK, :] = late * early_decay[h : h + 1, :] + early


def place_of(c):
    return sum(((c >> (4 - CHIP_BITS.index(name))) & 1) << (4 - i) for i, name in enumerate(EXCHANGE))


def scan_forward_kernel(in_ref, out_ref, decay_ref):
    state = jnp.zeros((PART, LANES), F32)
    for c in range(CHIPS):
        place = place_of(c)
        out_ref[PART * place : PART * place + PART, :] = state
        at = FWD_PART * place
        decay = in_ref[at + PART : at + PART + 1, :]
        decay_ref[c : c + 1, :] = decay
        state = state * decay + in_ref[at : at + PART, :]


def scan_backward_kernel(in_ref, decay_ref, after_ref, after_too_ref, out_ref):
    state = jnp.zeros((PART, LANES), F32)
    for c in reversed(range(CHIPS)):
        at = PART * place_of(c)
        out_ref[at : at + PART, :] = state
        state = state * decay_ref[c : c + 1, :] + in_ref[at : at + PART, :]


def step_kernel(core_ref, stepping, state_ref, add_ref, decay_ref, out_ref):
    steps = core_ref[0] == stepping
    for h in range(HALF):
        at = slice(PACK * h, PACK * h + PACK)
        state = state_ref[at, :]
        stepped = state * decay_ref[HALF_ROWS + h : HALF_ROWS + h + 1, :] + add_ref[at, :]
        out_ref[at, :] = jnp.where(steps, stepped, state)


def step_forward_kernel(core_ref, state_ref, x_ref, out_ref):
    step_kernel(core_ref, 0, state_ref, x_ref, x_ref, out_ref)


def step_backward_kernel(core_ref, state_ref, c_ref, x_ref, out_ref):
    step_kernel(core_ref, 1, state_ref, c_ref, x_ref, out_ref)


def own_states(core, late, own_ref, add_ref, decay_ref, out_ref):
    for h in range(HALF):
        at = slice(PACK * h, PACK * h + PACK)
        own = own_ref[at, :]
        stepped = own * decay_ref[HALF_ROWS + h : HALF_ROWS + h + 1, :] + add_ref[at, :]
        out_ref[at, :] = jnp.where(core == late, stepped, own)


def add_tiles(tiles, part, j):
    for i in range(SPAN[j] // LANES):
        t = START[j] // LANES + i
        piece = part[:, LANES * i : LANES * i + LANES]
        tiles[t] = piece if tiles[t] is None else tiles[t] + piece


def keys_of(kv_ref):
    return kv_ref.at[pl.ds(0, TOKENS)]


def values_of(kv_ref):
    return kv_ref.at[pl.ds(TOKENS, TOKENS)]


def group_lanes(half, i):
    return at_lanes(384 * (2 * half + i), 0, 384)


def inner_half(half, q_ref, kv_ref, accum_ref, inner_ref, start_ref):
    accum = half_rows(accum_ref, half)
    cols = columns(accum)
    start_ref[...] = jnp.exp(cols)
    k_ref, v_ref = keys_of(kv_ref), values_of(kv_ref)
    for i in range(2):
        g = 2 * half + i
        tiles = [None] * 3
        for j in range(4):
            scores = dot_nt(head_tiles(q_ref, g, j, True), head_tiles(k_ref, g, j, False))
            weights = (scores * weight_of(accum, cols, 4 * i + j)).astype(BF16)
            add_tiles(tiles, dot_nn(weights, head_tiles(v_ref, g, j, True)), j)
        for t in range(3):
            inner_ref[:, 384 * i + LANES * t : 384 * i + LANES * t + LANES] = tiles[t]


def inner_kernel(
    core_ref, q_ref, kv_ref, accum_ref,
    own_inner_ref, own_start_ref, inner_ref, start_ref,
):
    core = core_ref[0]
    inner_half(core, q_ref, kv_ref, accum_ref, own_inner_ref, own_start_ref)
    inner_half(1 - core, q_ref, kv_ref, accum_ref, inner_ref, start_ref)


def attention_half(half, q_ref, y_ref, gain_ref, start_ref, inner_ref, state_ref, o_ref, squares, crossed):
    start = start_ref[...]
    for i in range(2):
        pairs = [pair_states(state_ref, i, p) for p in range(2)]
        lanes = group_lanes(half, i)
        at = slice(384 * i, 384 * i + 384)
        attention = inner_ref[:, at] + group_columns(start, i) * times_states(q_ref[:, lanes], pairs, dot_nn)
        o_ref[:, at] = attention
        both = gain_ref[:, lanes] * y_ref[:, lanes].astype(F32) * attention
        square = attention * attention
        for t in range(3):
            squares = squares + square[:, LANES * t : LANES * t + LANES]
            crossed = crossed + both[:, LANES * t : LANES * t + LANES]
    return squares, crossed


def attention_kernel(
    core_ref, q_ref, y_ref, gain_ref, own_start_ref, own_inner_ref, start_ref, inner_ref, own_ref, got_ref, got_x_ref,
    own_o_ref, other_o_ref, sums_ref, state_ref,
):
    core = core_ref[0]
    own_states(core, 1, own_ref, got_x_ref, got_x_ref, state_ref)
    zero = jnp.zeros((TOKENS, LANES), F32)
    squares, crossed = attention_half(
        core, q_ref, y_ref, gain_ref, own_start_ref, own_inner_ref, state_ref, own_o_ref, zero, zero
    )
    squares, crossed = attention_half(
        1 - core, q_ref, y_ref, gain_ref, start_ref, inner_ref, got_ref, other_o_ref, squares, crossed
    )
    sums_ref[0:1, :] = jnp.sum(squares.T, axis=0, keepdims=True)
    sums_ref[1:2, :] = jnp.sum(crossed.T, axis=0, keepdims=True)


def norm_kernel(
    core_ref, q_ref, y_ref, gain_ref, accum_ref, own_o_ref, other_o_ref, sums_0, sums_1, sums_2, sums_3, back_ref, c_ref
):
    sums = (sums_0[...] + sums_1[...]) + (sums_2[...] + sums_3[...])
    root = jnp.sqrt(sums[0:1, :] / (HEADS * HEAD_DIM) + 1e-05)
    factor = sums[1:2, :] / (HEADS * HEAD_DIM * root * root * root)
    cols = columns(jnp.concatenate([1.0 / root, factor], axis=0))
    inverse = jnp.broadcast_to(cols[:, 0:1], (TOKENS, 384))
    factor = jnp.broadcast_to(cols[:, 1:2], (TOKENS, 384))
    core = core_ref[0]
    for half, o_ref in ((1 - core, other_o_ref), (core, own_o_ref)):
        for i in range(2):
            lanes = group_lanes(half, i)
            scaled = gain_ref[:, lanes] * y_ref[:, lanes].astype(F32)
            back_ref[:, lanes] = (scaled * inverse - o_ref[:, 384 * i : 384 * i + 384] * factor).astype(BF16)
    half = 1 - core
    outer_states(half, q_ref, jnp.exp(half_rows(accum_ref, half)), back_ref, c_ref)


def carry_keep_kernel(core_ref, q_ref, back_ref, accum_ref, c_ref):
    half = core_ref[0]
    outer_states(half, q_ref, jnp.exp(half_rows(accum_ref, half)), back_ref, c_ref)


def middle_half(half, q_ref, kv_ref, back_ref, accum_ref, state_ref, gq_ref, gk_ref, tail_ref):
    accum = half_rows(accum_ref, half)
    tail_ref[...] = columns(jnp.exp(accum[:, LANES - 1 :] - accum))
    cols = columns(accum)
    start = jnp.exp(cols)
    k_ref, v_ref = keys_of(kv_ref), values_of(kv_ref)
    for i in range(2):
        g = 2 * half + i
        pairs = [pair_states(state_ref, i, p) for p in range(2)]
        gq = group_columns(start, i) * times_states(back_ref[:, group_lanes(half, i)], pairs, dot_nt)
        gq = [gq[:, LANES * t : LANES * t + LANES] for t in range(3)]
        gk = [None] * 3
        for j in range(4):
            h = 4 * i + j
            q = head_tiles(q_ref, g, j, True)
            k = head_tiles(k_ref, g, j, True)
            v = head_tiles(v_ref, g, j, False)
            d = head_tiles(back_ref, g, j, True)
            weights = (dot_nt(d, v) * weight_of(accum, cols, h)).astype(BF16)
            weights_t = (dot_nt(v, d) * weight_turned(accum, cols, h)).astype(BF16)
            add_tiles(gq, dot_nn(weights, k), j)
            add_tiles(gk, dot_nn(weights_t, q), j)
        for t in range(3):
            gq_ref[:, at_lanes(384 * g, LANES * t, LANES)] = gq[t].astype(BF16)
            gk_ref[:, 384 * i + LANES * t : 384 * i + LANES * t + LANES] = gk[t]


def middle_kernel(
    core_ref, q_ref, kv_ref, back_ref, accum_ref, own_ref, got_x_ref, other_state_ref,
    gq_ref, own_gk_ref, other_gk_ref, own_tail_ref, tail_ref, done_ref, own_state_ref,
):
    done_ref[...] = accum_ref[0:8, :]
    core = core_ref[0]
    own_states(core, 1, own_ref, got_x_ref, got_x_ref, own_state_ref)
    middle_half(core, q_ref, kv_ref, back_ref, accum_ref, own_state_ref, gq_ref, own_gk_ref, own_tail_ref)
    middle_half(1 - core, q_ref, kv_ref, back_ref, accum_ref, other_state_ref, gq_ref, other_gk_ref, tail_ref)


def values_half(half, q_ref, kv_ref, back_ref, accum_ref, gv_ref):
    accum = half_rows(accum_ref, half)
    cols = columns(accum)
    k_ref = keys_of(kv_ref)
    for i in range(2):
        g = 2 * half + i
        gv = [None] * 3
        for j in range(4):
            scores = dot_nt(head_tiles(k_ref, g, j, True), head_tiles(q_ref, g, j, False))
            weights = (scores * weight_turned(accum, cols, 4 * i + j)).astype(BF16)
            add_tiles(gv, dot_nn(weights, head_tiles(back_ref, g, j, True)), j)
        for t in range(3):
            gv_ref[:, 384 * i + LANES * t : 384 * i + LANES * t + LANES] = gv[t]


def values_own_kernel(core_ref, q_ref, kv_ref, back_ref, accum_ref, gv_ref, done_ref):
    done_ref[...] = accum_ref[0:8, :]
    values_half(core_ref[0], q_ref, kv_ref, back_ref, accum_ref, gv_ref)


def values_other_kernel(core_ref, q_ref, kv_ref, back_ref, accum_ref, gv_ref):
    values_half(1 - core_ref[0], q_ref, kv_ref, back_ref, accum_ref, gv_ref)


def last_group(half, i, kv_ref, tail, gk0_ref, gv0_ref, carry_ref, gk_ref, gv_ref):
    pairs = [pair_states(carry_ref, i, p) for p in range(2)]
    lanes = group_lanes(half, i)
    at = slice(384 * i, 384 * i + 384)
    wide = group_columns(tail, i)
    k_ref, v_ref = keys_of(kv_ref), values_of(kv_ref)
    gk_ref[:, at] = (gk0_ref[:, at] + wide * times_states(v_ref[:, lanes], pairs, dot_nt)).astype(BF16)
    gv_ref[:, at] = (gv0_ref[:, at] + wide * times_states(k_ref[:, lanes], pairs, dot_nn)).astype(BF16)


def last_own_kernel(
    core_ref, kv_ref, tail_ref, gk0_ref, gv0_ref, own_ref, got_c_ref, got_x_ref, gk_ref, gv_ref, carry_ref
):
    core = core_ref[0]
    own_states(core, 0, own_ref, got_c_ref, got_x_ref, carry_ref)
    for i in range(2):
        last_group(core, i, kv_ref, tail_ref[...], gk0_ref, gv0_ref, carry_ref, gk_ref, gv_ref)


def last_other_kernel(
    core_ref, kv_ref, tail_ref, gk0_ref, gv0_ref, carry_ref, own_gk_ref, own_gv_ref,
    gk_hbm, gv_hbm, gk_ref, gv_ref, sems,
):
    core = core_ref[0]
    copies = []

    def copy_out(half, i, gk, gv, first):
        lanes = group_lanes(half, i)
        for n, (src, dst) in enumerate(((gk, gk_hbm), (gv, gv_hbm))):
            copy = pltpu.make_async_copy(src.at[:, pl.ds(384 * i, 384)], dst.at[:, lanes], sems.at[first + n])
            copy.start()
            copies.append(copy)

    for i in range(2):
        copy_out(core, i, own_gk_ref, own_gv_ref, 2 * i)
    for i in range(2):
        last_group(1 - core, i, kv_ref, tail_ref[...], gk0_ref, gv0_ref, carry_ref, gk_ref, gv_ref)
        copy_out(1 - core, i, gk_ref, gv_ref, 4 + 2 * i)
    for copy in copies:
        copy.wait()


def call(kernel, outs, smem, *args, hbm_in=(), hbm_out=(), scratch=(), flops=0):
    specs = []
    for i, arg in enumerate(args):
        space = pltpu.SMEM if i < smem else pltpu.HBM if i in hbm_in else pltpu.VMEM
        specs.append(pl.BlockSpec(memory_space=space))
    shapes = [jax.ShapeDtypeStruct(s, d) for s, d in outs]
    moved = sum(a.size * a.dtype.itemsize for a in args) + sum(s.size * s.dtype.itemsize for s in shapes)
    out = pl.pallas_call(
        kernel,
        out_shape=shapes,
        in_specs=specs,
        out_specs=[pl.BlockSpec(memory_space=pltpu.HBM if i in hbm_out else pltpu.VMEM) for i in range(len(shapes))],
        scratch_shapes=scratch,
        compiler_params=pltpu.CompilerParams(vmem_limit_bytes=VMEM),
        cost_estimate=pl.CostEstimate(flops=flops, bytes_accessed=moved, transcendentals=0),
        name=kernel.__name__,
    )(*args)
    return out[0] if len(out) == 1 else out


SWAP = [(0, 1), (1, 0)]
CHIP_BITS = ("xh", "xl", "zh", "zm", "zl")
EXCHANGE = ("zm", "zh", "xh", "zl", "xl")


def swap(value):
    return lax.ppermute(value, "core", SWAP)


def exchange(value):
    rows = value.shape[0] // CHIPS
    parts = value.reshape(CHIPS, rows // 2, 2, LANES) if rows % 2 == 0 else value.reshape(-1)
    return lax.all_to_all(parts, EXCHANGE, 0, 0, tiled=True).reshape(value.shape)


def others(value):
    return [lax.ppermute(value, "head", [(i, (i + k) % 4) for i in range(4)]) for k in (1, 2, 3)]


def local(q, k, v, y, logs, gain):
    core = lax.axis_index("core").astype(jnp.int32).reshape(1)
    gain = gain.reshape(1, WIDTH)
    half = ((HALF_ROWS, LANES), F32)
    half_decay = ((HALF_ROWS + HALF, LANES), F32)
    rows = ((LOCAL_HEADS, LANES), F32)
    cols = ((TOKENS, LANES), F32)
    token = ((8, LANES), F32)
    wide = (TOKENS, WIDTH)
    half_wide = ((TOKENS, WIDTH // 2), F32)
    narrow = pltpu.VMEM((TOKENS, WIDTH // 2), BF16)
    kv, logs = lax.optimization_barrier((jnp.concatenate([k, v]), logs))
    x_send, accum = call(state_send_kernel, [half_decay, rows], 1, core, kv, logs, flops=10**9)
    got_x = swap(x_send)
    x_keep = call(state_keep_kernel, [half_decay], 1, core, kv, accum, flops=10**9)
    payload = call(
        combine_forward_kernel, [((CHIPS * FWD_PART, LANES), F32)], 1, core, x_keep, got_x
    )
    payload = exchange(payload)
    entering, decays = call(scan_forward_kernel, [half, ((CHIPS, LANES), F32)], 0, payload)
    entering = exchange(entering)
    got_entering = swap(call(step_forward_kernel, [half], 1, core, entering, x_keep))
    own_inner, own_start, inner, start = call(
        inner_kernel, [half_wide, cols, half_wide, cols], 1, core, q, kv, accum, flops=2 * 10**9
    )
    half_scratch = pltpu.VMEM((HALF_ROWS, LANES), F32)
    own_o, other_o, sums = call(
        attention_kernel,
        [half_wide, half_wide, ((2, LANES), F32)],
        1, core, q, y, gain, own_start, own_inner, start, inner, entering, got_entering, got_x,
        scratch=[half_scratch],
        flops=10**9,
    )
    back, c_send = call(
        norm_kernel,
        [(wide, BF16), half],
        1, core, q, y, gain, accum, own_o, other_o, sums, *others(sums),
        flops=10**9,
    )
    got_c = swap(c_send)
    c_keep = call(carry_keep_kernel, [half], 1, core, q, back, accum, flops=5 * 10**8)
    own_gv, values_done = call(values_own_kernel, [half_wide, token], 1, core, q, kv, back, accum, flops=10**9)
    payload = call(combine_backward_kernel, [half], 1, core, c_keep, got_c, x_keep, got_x)
    payload = exchange(payload)
    gq, own_gk, other_gk, own_tail, tail, middle_done = call(
        middle_kernel,
        [(wide, BF16), half_wide, half_wide, cols, cols, token],
        1, core, q, kv, back, accum, entering, got_x, got_entering,
        scratch=[half_scratch],
        flops=4 * 10**9,
    )
    leaving = call(scan_backward_kernel, [half], 0, payload, decays, middle_done, values_done)
    leaving = exchange(leaving)
    got_leaving = swap(call(step_backward_kernel, [half], 1, core, leaving, c_keep, x_keep))
    other_gv = call(values_other_kernel, [half_wide], 1, core, q, kv, back, accum, flops=10**9)
    half_narrow = ((TOKENS, WIDTH // 2), BF16)
    own_gk, own_gv = call(
        last_own_kernel,
        [half_narrow, half_narrow],
        1, core, kv, own_tail, own_gk, own_gv, leaving, got_c, got_x,
        scratch=[half_scratch],
        flops=5 * 10**8,
    )
    gk, gv = call(
        last_other_kernel,
        [(wide, BF16), (wide, BF16)],
        1, core, kv, tail, other_gk, other_gv, got_leaving, own_gk, own_gv,
        hbm_out=(0, 1),
        scratch=[narrow, narrow, pltpu.SemaphoreType.DMA((8,))],
        flops=5 * 10**8,
    )
    return gq, gk, gv


def solution(mesh):
    tokens = (*CHIP_BITS, "core")
    grid = Mesh(mesh.devices.reshape(2, 2, 2, 2, 2, 2, 4), (*tokens, "head"))
    rows = P(tokens, "head")
    return jax.shard_map(
        local,
        mesh=grid,
        in_specs=(rows, rows, rows, rows, P("head", tokens), P("head")),
        out_specs=(rows, rows, rows),
        check_vma=False,
    )
```

```python
import jax
import jax.numpy as jnp
from jax import lax
from jax.experimental import pallas as pl
from jax.experimental.pallas import tpu as pltpu
from jax.sharding import Mesh, PartitionSpec as P

HEADS = 64
HEAD_DIM = 96
TOKENS = 128
LOCAL_HEADS = 16
HALF = 8
WIDTH = LOCAL_HEADS * HEAD_DIM
LANES = 128
PACK = 72
CHIPS = 32
PART = 18
FWD_PART = 19
ROWS = LOCAL_HEADS * PACK
HALF_ROWS = HALF * PACK
VMEM = 12 * 1024 * 1024

F32 = jnp.float32
BF16 = jnp.bfloat16

START = (0, 0, 128, 256)
SPAN = (128, 256, 256, 128)
FIRST = (0, 96, 64, 32)
FREE = (3, 2, 1, 0)


def lanes_of(shape):
    return lax.broadcasted_iota(jnp.int32, shape, len(shape) - 1)


def rows_of(shape):
    return lax.broadcasted_iota(jnp.int32, shape, len(shape) - 2)


def dot_nn(a, b):
    return lax.dot_general(a, b, (((1,), (0,)), ((), ())), preferred_element_type=F32)


def dot_nt(a, b):
    return lax.dot_general(a, b, (((1,), (1,)), ((), ())), preferred_element_type=F32)


def two(x):
    high = x.astype(BF16)
    return high, (x - high.astype(F32)).astype(BF16)


def at_lanes(base, start, size):
    return pl.ds(base + start if isinstance(base, int) else pl.multiple_of(base + start, LANES), size)


def head_tiles(value, g, j, masked):
    part = value[:, at_lanes(384 * g, START[j], SPAN[j])]
    if masked:
        lane = lanes_of(part.shape)
        part = jnp.where((lane >= FIRST[j]) & (lane < FIRST[j] + HEAD_DIM), part, jnp.zeros_like(part))
    return part


def merge(tiles):
    return tiles if tiles.shape[1] == LANES else tiles[:, :LANES] + tiles[:, LANES:]


def pack(square, j):
    lane = lanes_of((24, LANES))
    free = lane // 32 == FREE[j]
    extra = square[PACK:]
    others = [c for c in range(4) if c != FREE[j]]
    return [
        jnp.where(free, pltpu.roll(extra, (32 * (FREE[j] - c)) % LANES, 1), square[24 * i : 24 * i + 24])
        for i, c in enumerate(others)
    ]


def unpack(packed, j):
    lane = lanes_of((24, LANES))
    others = [c for c in range(4) if c != FREE[j]]
    extra = jnp.zeros((24, LANES), F32)
    for i, c in enumerate(others):
        moved = pltpu.roll(packed[24 * i : 24 * i + 24], (32 * (c - FREE[j])) % LANES, 1)
        extra = jnp.where(lane // 32 == c, moved, extra)
    return jnp.concatenate([packed, extra], axis=0)


def spread(square, j):
    lane = lanes_of(square.shape)
    zero = jnp.zeros_like(square)
    if j == 0:
        tiles = (jnp.where(lane < 96, square, zero), zero)
    elif j == 1:
        tiles = (jnp.where(lane >= 96, square, zero), jnp.where(lane < 64, square, zero))
    elif j == 2:
        tiles = (jnp.where(lane >= 64, square, zero), jnp.where(lane < 32, square, zero))
    else:
        tiles = (zero, jnp.where(lane >= 32, square, zero))
    return jnp.concatenate(tiles, axis=1)


def pair_states(ref, g, pair):
    parts = []
    for j in (2 * pair, 2 * pair + 1):
        h = 4 * g + j
        parts.append([spread(part, j) for part in two(unpack(ref[PACK * h : PACK * h + PACK, :], j))])
    zero = jnp.zeros((64, 256), BF16)
    out = []
    for first, second in zip(*parts):
        rows = [first, second, zero] if pair == 0 else [zero, first, second]
        out.append(jnp.concatenate(rows, axis=0))
    return out


def times_states(values, pairs, dot):
    left, right = (
        dot(values[:, LANES * p : LANES * p + 256], pairs[p][0])
        + dot(values[:, LANES * p : LANES * p + 256], pairs[p][1])
        for p in range(2)
    )
    return jnp.concatenate([left[:, :LANES], left[:, LANES:] + right[:, :LANES], right[:, LANES:]], axis=1)


def running(logs):
    high = logs.astype(BF16)
    rest = logs - high.astype(F32)
    middle = rest.astype(BF16)
    low = (rest - middle.astype(F32)).astype(BF16)
    shape = (LANES, LANES)
    upto = jnp.where(rows_of(shape) <= lanes_of(shape), 1.0, 0.0).astype(BF16)
    return dot_nn(low, upto) + dot_nn(middle, upto) + dot_nn(high, upto)


def columns(rows):
    filler = jnp.zeros((LANES - rows.shape[0], LANES), F32)
    return jnp.concatenate([rows, filler], axis=0).T


def wide_column(cols, h):
    return jnp.broadcast_to(cols[:, h : h + 1], (TOKENS, LANES))


def group_columns(cols, g):
    lane = lanes_of((TOKENS, LANES))
    c = [wide_column(cols, 4 * g + j) for j in range(4)]
    return jnp.concatenate(
        [jnp.where(lane < 96, c[0], c[1]), jnp.where(lane < 64, c[1], c[2]), jnp.where(lane < 32, c[2], c[3])],
        axis=1,
    )


def weight_of(accum, cols, h):
    row = accum[h : h + 1, :]
    spread_by = wide_column(cols, h) - row
    shape = (TOKENS, LANES)
    keep = lanes_of(shape) <= rows_of(shape)
    return jnp.exp(jnp.where(keep, spread_by, -jnp.inf))


def weight_turned(accum, cols, h):
    spread_by = accum[h : h + 1, :] - wide_column(cols, h)
    shape = (TOKENS, LANES)
    keep = rows_of(shape) <= lanes_of(shape)
    return jnp.exp(jnp.where(keep, spread_by, -jnp.inf))


def outer_states(half, left_ref, scale, right_ref, out_ref):
    for i in range(2):
        g = 2 * half + i
        turned = left_ref[:, at_lanes(384 * g, 0, 384)].astype(F32).T
        for j in range(4):
            h = 4 * i + j
            left = jnp.concatenate(two(turned[96 * j : 96 * j + 96, :] * scale[h : h + 1, :]), axis=0)
            both = dot_nn(left, head_tiles(right_ref, g, j, True))
            square = merge(both[:96] + both[96:])
            for n, piece in enumerate(pack(square, j)):
                out_ref[PACK * h + 24 * n : PACK * h + 24 * n + 24, :] = piece


def half_rows(ref, half):
    return ref[pl.ds(pl.multiple_of(HALF * half, HALF), HALF), :]


def state_half(half, kv_ref, accum_ref, out_ref):
    accum = half_rows(accum_ref, half)
    last = jnp.broadcast_to(accum[:, LANES - 1 :], (HALF, LANES))
    out_ref[HALF_ROWS : HALF_ROWS + HALF, :] = jnp.exp(last)
    keys, values = kv_ref.at[pl.ds(0, TOKENS)], kv_ref.at[pl.ds(TOKENS, TOKENS)]
    outer_states(half, keys, jnp.exp(last - accum), values, out_ref)


def state_send_kernel(core_ref, kv_ref, logs_ref, out_ref, accum_ref):
    accum_ref[...] = running(logs_ref[...])
    state_half(1 - core_ref[0], kv_ref, accum_ref, out_ref)


def state_keep_kernel(core_ref, kv_ref, accum_ref, out_ref):
    state_half(core_ref[0], kv_ref, accum_ref, out_ref)


def combine_forward_kernel(core_ref, own_ref, got_ref, out_ref):
    first = core_ref[0] == 0
    own_decay = own_ref[HALF_ROWS : HALF_ROWS + HALF, :]
    got_decay = got_ref[HALF_ROWS : HALF_ROWS + HALF, :]
    late_decay = jnp.where(first, got_decay, own_decay)
    both_decay = own_decay * got_decay
    for h in range(HALF):
        own = own_ref[PACK * h : PACK * h + PACK, :]
        got = got_ref[PACK * h : PACK * h + PACK, :]
        early = jnp.where(first, own, got)
        late = jnp.where(first, got, own)
        total = early * late_decay[h : h + 1, :] + late
        for quarter in range(4):
            to = FWD_PART * (4 * h + quarter)
            out_ref[to : to + PART, :] = total[PART * quarter : PART * quarter + PART, :]
            out_ref[to + PART : to + FWD_PART, :] = both_decay[h : h + 1, :]


def combine_backward_kernel(core_ref, own_ref, got_ref, own_x_ref, got_x_ref, out_ref):
    first = core_ref[0] == 0
    at = slice(HALF_ROWS, HALF_ROWS + HALF)
    early_decay = jnp.where(first, own_x_ref[at, :], got_x_ref[at, :])
    for h in range(HALF):
        own = own_ref[PACK * h : PACK * h + PACK, :]
        got = got_ref[PACK * h : PACK * h + PACK, :]
        early = jnp.where(first, own, got)
        late = jnp.where(first, got, own)
        out_ref[PACK * h : PACK * h + PACK, :] = late * early_decay[h : h + 1, :] + early


def place_of(c):
    return sum(((c >> (4 - CHIP_BITS.index(name))) & 1) << (4 - i) for i, name in enumerate(EXCHANGE))


def scan_forward_kernel(in_ref, out_ref, decay_ref):
    state = jnp.zeros((PART, LANES), F32)
    for c in range(CHIPS):
        place = place_of(c)
        out_ref[PART * place : PART * place + PART, :] = state
        at = FWD_PART * place
        decay = in_ref[at + PART : at + PART + 1, :]
        decay_ref[c : c + 1, :] = decay
        state = state * decay + in_ref[at : at + PART, :]


def scan_backward_kernel(in_ref, decay_ref, after_ref, after_too_ref, out_ref):
    state = jnp.zeros((PART, LANES), F32)
    for c in reversed(range(CHIPS)):
        at = PART * place_of(c)
        out_ref[at : at + PART, :] = state
        state = state * decay_ref[c : c + 1, :] + in_ref[at : at + PART, :]


def step_kernel(core_ref, stepping, state_ref, add_ref, decay_ref, out_ref):
    steps = core_ref[0] == stepping
    for h in range(HALF):
        at = slice(PACK * h, PACK * h + PACK)
        state = state_ref[at, :]
        stepped = state * decay_ref[HALF_ROWS + h : HALF_ROWS + h + 1, :] + add_ref[at, :]
        out_ref[at, :] = jnp.where(steps, stepped, state)


def step_forward_kernel(core_ref, state_ref, x_ref, out_ref):
    step_kernel(core_ref, 0, state_ref, x_ref, x_ref, out_ref)


def step_backward_kernel(core_ref, state_ref, c_ref, x_ref, out_ref):
    step_kernel(core_ref, 1, state_ref, c_ref, x_ref, out_ref)


def own_states(core, late, own_ref, add_ref, decay_ref, out_ref):
    for h in range(HALF):
        at = slice(PACK * h, PACK * h + PACK)
        own = own_ref[at, :]
        stepped = own * decay_ref[HALF_ROWS + h : HALF_ROWS + h + 1, :] + add_ref[at, :]
        out_ref[at, :] = jnp.where(core == late, stepped, own)


def add_tiles(tiles, part, j):
    for i in range(SPAN[j] // LANES):
        t = START[j] // LANES + i
        piece = part[:, LANES * i : LANES * i + LANES]
        tiles[t] = piece if tiles[t] is None else tiles[t] + piece


def keys_of(kv_ref):
    return kv_ref.at[pl.ds(0, TOKENS)]


def values_of(kv_ref):
    return kv_ref.at[pl.ds(TOKENS, TOKENS)]


def group_lanes(half, i):
    return at_lanes(384 * (2 * half + i), 0, 384)


def inner_half(half, q_ref, kv_ref, accum_ref, inner_ref, start_ref):
    accum = half_rows(accum_ref, half)
    cols = columns(accum)
    start_ref[...] = jnp.exp(cols)
    k_ref, v_ref = keys_of(kv_ref), values_of(kv_ref)
    for i in range(2):
        g = 2 * half + i
        tiles = [None] * 3
        for j in range(4):
            scores = dot_nt(head_tiles(q_ref, g, j, True), head_tiles(k_ref, g, j, False))
            weights = (scores * weight_of(accum, cols, 4 * i + j)).astype(BF16)
            add_tiles(tiles, dot_nn(weights, head_tiles(v_ref, g, j, True)), j)
        for t in range(3):
            inner_ref[:, 384 * i + LANES * t : 384 * i + LANES * t + LANES] = tiles[t]


def inner_kernel(
    core_ref, q_ref, kv_ref, accum_ref,
    own_inner_ref, own_start_ref, inner_ref, start_ref,
):
    core = core_ref[0]
    inner_half(core, q_ref, kv_ref, accum_ref, own_inner_ref, own_start_ref)
    inner_half(1 - core, q_ref, kv_ref, accum_ref, inner_ref, start_ref)


def attention_half(half, q_ref, y_ref, gain_ref, start_ref, inner_ref, state_ref, o_ref, squares, crossed):
    start = start_ref[...]
    for i in range(2):
        pairs = [pair_states(state_ref, i, p) for p in range(2)]
        lanes = group_lanes(half, i)
        at = slice(384 * i, 384 * i + 384)
        attention = inner_ref[:, at] + group_columns(start, i) * times_states(q_ref[:, lanes], pairs, dot_nn)
        o_ref[:, at] = attention
        both = gain_ref[:, lanes] * y_ref[:, lanes].astype(F32) * attention
        square = attention * attention
        for t in range(3):
            squares = squares + square[:, LANES * t : LANES * t + LANES]
            crossed = crossed + both[:, LANES * t : LANES * t + LANES]
    return squares, crossed


def attention_kernel(
    core_ref, q_ref, y_ref, gain_ref, own_start_ref, own_inner_ref, start_ref, inner_ref, own_ref, got_ref, got_x_ref,
    own_o_ref, other_o_ref, sums_ref, state_ref,
):
    core = core_ref[0]
    own_states(core, 1, own_ref, got_x_ref, got_x_ref, state_ref)
    zero = jnp.zeros((TOKENS, LANES), F32)
    squares, crossed = attention_half(
        core, q_ref, y_ref, gain_ref, own_start_ref, own_inner_ref, state_ref, own_o_ref, zero, zero
    )
    squares, crossed = attention_half(
        1 - core, q_ref, y_ref, gain_ref, start_ref, inner_ref, got_ref, other_o_ref, squares, crossed
    )
    sums_ref[0:1, :] = jnp.sum(squares.T, axis=0, keepdims=True)
    sums_ref[1:2, :] = jnp.sum(crossed.T, axis=0, keepdims=True)


def norm_kernel(
    core_ref, q_ref, y_ref, gain_ref, accum_ref, own_o_ref, other_o_ref, sums_0, sums_1, sums_2, sums_3, back_ref, c_ref
):
    sums = (sums_0[...] + sums_1[...]) + (sums_2[...] + sums_3[...])
    root = jnp.sqrt(sums[0:1, :] / (HEADS * HEAD_DIM) + 1e-05)
    factor = sums[1:2, :] / (HEADS * HEAD_DIM * root * root * root)
    cols = columns(jnp.concatenate([1.0 / root, factor], axis=0))
    inverse = jnp.broadcast_to(cols[:, 0:1], (TOKENS, 384))
    factor = jnp.broadcast_to(cols[:, 1:2], (TOKENS, 384))
    core = core_ref[0]
    for half, o_ref in ((1 - core, other_o_ref), (core, own_o_ref)):
        for i in range(2):
            lanes = group_lanes(half, i)
            scaled = gain_ref[:, lanes] * y_ref[:, lanes].astype(F32)
            back_ref[:, lanes] = (scaled * inverse - o_ref[:, 384 * i : 384 * i + 384] * factor).astype(BF16)
    half = 1 - core
    outer_states(half, q_ref, jnp.exp(half_rows(accum_ref, half)), back_ref, c_ref)


def carry_keep_kernel(core_ref, q_ref, back_ref, accum_ref, c_ref):
    half = core_ref[0]
    outer_states(half, q_ref, jnp.exp(half_rows(accum_ref, half)), back_ref, c_ref)


def middle_half(half, q_ref, kv_ref, back_ref, accum_ref, state_ref, gq_ref, gk_ref, tail_ref):
    accum = half_rows(accum_ref, half)
    tail_ref[...] = columns(jnp.exp(accum[:, LANES - 1 :] - accum))
    cols = columns(accum)
    start = jnp.exp(cols)
    k_ref, v_ref = keys_of(kv_ref), values_of(kv_ref)
    for i in range(2):
        g = 2 * half + i
        pairs = [pair_states(state_ref, i, p) for p in range(2)]
        gq = group_columns(start, i) * times_states(back_ref[:, group_lanes(half, i)], pairs, dot_nt)
        gq = [gq[:, LANES * t : LANES * t + LANES] for t in range(3)]
        gk = [None] * 3
        for j in range(4):
            h = 4 * i + j
            q = head_tiles(q_ref, g, j, True)
            k = head_tiles(k_ref, g, j, True)
            v = head_tiles(v_ref, g, j, False)
            d = head_tiles(back_ref, g, j, True)
            weights = (dot_nt(d, v) * weight_of(accum, cols, h)).astype(BF16)
            weights_t = (dot_nt(v, d) * weight_turned(accum, cols, h)).astype(BF16)
            add_tiles(gq, dot_nn(weights, k), j)
            add_tiles(gk, dot_nn(weights_t, q), j)
        for t in range(3):
            gq_ref[:, at_lanes(384 * g, LANES * t, LANES)] = gq[t].astype(BF16)
            gk_ref[:, 384 * i + LANES * t : 384 * i + LANES * t + LANES] = gk[t]


def middle_kernel(
    core_ref, q_ref, kv_ref, back_ref, accum_ref, own_ref, got_x_ref, other_state_ref,
    gq_ref, own_gk_ref, other_gk_ref, own_tail_ref, tail_ref, done_ref, own_state_ref,
):
    done_ref[...] = accum_ref[0:8, :]
    core = core_ref[0]
    own_states(core, 1, own_ref, got_x_ref, got_x_ref, own_state_ref)
    middle_half(core, q_ref, kv_ref, back_ref, accum_ref, own_state_ref, gq_ref, own_gk_ref, own_tail_ref)
    middle_half(1 - core, q_ref, kv_ref, back_ref, accum_ref, other_state_ref, gq_ref, other_gk_ref, tail_ref)


def values_half(half, q_ref, kv_ref, back_ref, accum_ref, gv_ref):
    accum = half_rows(accum_ref, half)
    cols = columns(accum)
    k_ref = keys_of(kv_ref)
    for i in range(2):
        g = 2 * half + i
        gv = [None] * 3
        for j in range(4):
            scores = dot_nt(head_tiles(k_ref, g, j, True), head_tiles(q_ref, g, j, False))
            weights = (scores * weight_turned(accum, cols, 4 * i + j)).astype(BF16)
            add_tiles(gv, dot_nn(weights, head_tiles(back_ref, g, j, True)), j)
        for t in range(3):
            gv_ref[:, 384 * i + LANES * t : 384 * i + LANES * t + LANES] = gv[t]


def values_own_kernel(core_ref, q_ref, kv_ref, back_ref, accum_ref, gv_ref, done_ref):
    done_ref[...] = accum_ref[0:8, :]
    values_half(core_ref[0], q_ref, kv_ref, back_ref, accum_ref, gv_ref)


def values_other_kernel(core_ref, q_ref, kv_ref, back_ref, accum_ref, gv_ref):
    values_half(1 - core_ref[0], q_ref, kv_ref, back_ref, accum_ref, gv_ref)


def last_group(half, i, kv_ref, tail, gk0_ref, gv0_ref, carry_ref, gk_ref, gv_ref):
    pairs = [pair_states(carry_ref, i, p) for p in range(2)]
    lanes = group_lanes(half, i)
    at = slice(384 * i, 384 * i + 384)
    wide = group_columns(tail, i)
    k_ref, v_ref = keys_of(kv_ref), values_of(kv_ref)
    gk_ref[:, at] = (gk0_ref[:, at] + wide * times_states(v_ref[:, lanes], pairs, dot_nt)).astype(BF16)
    gv_ref[:, at] = (gv0_ref[:, at] + wide * times_states(k_ref[:, lanes], pairs, dot_nn)).astype(BF16)


def last_own_kernel(
    core_ref, kv_ref, tail_ref, gk0_ref, gv0_ref, own_ref, got_c_ref, got_x_ref, gk_ref, gv_ref, carry_ref
):
    core = core_ref[0]
    own_states(core, 0, own_ref, got_c_ref, got_x_ref, carry_ref)
    for i in range(2):
        last_group(core, i, kv_ref, tail_ref[...], gk0_ref, gv0_ref, carry_ref, gk_ref, gv_ref)


def last_other_kernel(
    core_ref, kv_ref, tail_ref, gk0_ref, gv0_ref, carry_ref, own_gk_ref, own_gv_ref,
    gk_hbm, gv_hbm, gk_ref, gv_ref, sems,
):
    core = core_ref[0]
    copies = []

    def copy_out(half, i, gk, gv, first):
        lanes = group_lanes(half, i)
        for n, (src, dst) in enumerate(((gk, gk_hbm), (gv, gv_hbm))):
            copy = pltpu.make_async_copy(src.at[:, pl.ds(384 * i, 384)], dst.at[:, lanes], sems.at[first + n])
            copy.start()
            copies.append(copy)

    for i in range(2):
        copy_out(core, i, own_gk_ref, own_gv_ref, 2 * i)
    for i in range(2):
        last_group(1 - core, i, kv_ref, tail_ref[...], gk0_ref, gv0_ref, carry_ref, gk_ref, gv_ref)
        copy_out(1 - core, i, gk_ref, gv_ref, 4 + 2 * i)
    for copy in copies:
        copy.wait()


def call(kernel, outs, smem, *args, hbm_in=(), hbm_out=(), scratch=(), flops=0):
    specs = []
    for i, arg in enumerate(args):
        space = pltpu.SMEM if i < smem else pltpu.HBM if i in hbm_in else pltpu.VMEM
        specs.append(pl.BlockSpec(memory_space=space))
    shapes = [jax.ShapeDtypeStruct(s, d) for s, d in outs]
    moved = sum(a.size * a.dtype.itemsize for a in args) + sum(s.size * s.dtype.itemsize for s in shapes)
    out = pl.pallas_call(
        kernel,
        out_shape=shapes,
        in_specs=specs,
        out_specs=[pl.BlockSpec(memory_space=pltpu.HBM if i in hbm_out else pltpu.VMEM) for i in range(len(shapes))],
        scratch_shapes=scratch,
        compiler_params=pltpu.CompilerParams(vmem_limit_bytes=VMEM),
        cost_estimate=pl.CostEstimate(flops=flops, bytes_accessed=moved, transcendentals=0),
        name=kernel.__name__,
    )(*args)
    return out[0] if len(out) == 1 else out


SWAP = [(0, 1), (1, 0)]
CHIP_BITS = ("xh", "xl", "zh", "zm", "zl")
EXCHANGE = ("zm", "zh", "xh", "zl", "xl")


def swap(value):
    return lax.ppermute(value, "core", SWAP)


def exchange(value):
    rows = value.shape[0] // CHIPS
    parts = value.reshape(CHIPS, rows // 2, 2, LANES) if rows % 2 == 0 else value.reshape(-1)
    return lax.all_to_all(parts, EXCHANGE, 0, 0, tiled=True).reshape(value.shape)


def others(value):
    return [lax.ppermute(value, "head", [(i, i ^ k) for i in range(4)]) for k in (2, 1, 3)]


def local(q, k, v, y, logs, gain):
    core = lax.axis_index("core").astype(jnp.int32).reshape(1)
    gain = gain.reshape(1, WIDTH)
    half = ((HALF_ROWS, LANES), F32)
    half_decay = ((HALF_ROWS + HALF, LANES), F32)
    rows = ((LOCAL_HEADS, LANES), F32)
    cols = ((TOKENS, LANES), F32)
    token = ((8, LANES), F32)
    wide = (TOKENS, WIDTH)
    half_wide = ((TOKENS, WIDTH // 2), F32)
    narrow = pltpu.VMEM((TOKENS, WIDTH // 2), BF16)
    kv, logs = lax.optimization_barrier((jnp.concatenate([k, v]), logs))
    x_send, accum = call(state_send_kernel, [half_decay, rows], 1, core, kv, logs, flops=10**9)
    got_x = swap(x_send)
    x_keep = call(state_keep_kernel, [half_decay], 1, core, kv, accum, flops=10**9)
    payload = call(
        combine_forward_kernel, [((CHIPS * FWD_PART, LANES), F32)], 1, core, x_keep, got_x
    )
    payload = exchange(payload)
    entering, decays = call(scan_forward_kernel, [half, ((CHIPS, LANES), F32)], 0, payload)
    entering = exchange(entering)
    got_entering = swap(call(step_forward_kernel, [half], 1, core, entering, x_keep))
    own_inner, own_start, inner, start = call(
        inner_kernel, [half_wide, cols, half_wide, cols], 1, core, q, kv, accum, flops=2 * 10**9
    )
    half_scratch = pltpu.VMEM((HALF_ROWS, LANES), F32)
    own_o, other_o, sums = call(
        attention_kernel,
        [half_wide, half_wide, ((2, LANES), F32)],
        1, core, q, y, gain, own_start, own_inner, start, inner, entering, got_entering, got_x,
        scratch=[half_scratch],
        flops=10**9,
    )
    back, c_send = call(
        norm_kernel,
        [(wide, BF16), half],
        1, core, q, y, gain, accum, own_o, other_o, sums, *others(sums),
        flops=10**9,
    )
    got_c = swap(c_send)
    c_keep = call(carry_keep_kernel, [half], 1, core, q, back, accum, flops=5 * 10**8)
    own_gv, values_done = call(values_own_kernel, [half_wide, token], 1, core, q, kv, back, accum, flops=10**9)
    payload = call(combine_backward_kernel, [half], 1, core, c_keep, got_c, x_keep, got_x)
    payload = exchange(payload)
    gq, own_gk, other_gk, own_tail, tail, middle_done = call(
        middle_kernel,
        [(wide, BF16), half_wide, half_wide, cols, cols, token],
        1, core, q, kv, back, accum, entering, got_x, got_entering,
        scratch=[half_scratch],
        flops=4 * 10**9,
    )
    leaving = call(scan_backward_kernel, [half], 0, payload, decays, middle_done, values_done)
    leaving = exchange(leaving)
    got_leaving = swap(call(step_backward_kernel, [half], 1, core, leaving, c_keep, x_keep))
    other_gv = call(values_other_kernel, [half_wide], 1, core, q, kv, back, accum, flops=10**9)
    half_narrow = ((TOKENS, WIDTH // 2), BF16)
    own_gk, own_gv = call(
        last_own_kernel,
        [half_narrow, half_narrow],
        1, core, kv, own_tail, own_gk, own_gv, leaving, got_c, got_x,
        scratch=[half_scratch],
        flops=5 * 10**8,
    )
    gk, gv = call(
        last_other_kernel,
        [(wide, BF16), (wide, BF16)],
        1, core, kv, tail, other_gk, other_gv, got_leaving, own_gk, own_gv,
        hbm_out=(0, 1),
        scratch=[narrow, narrow, pltpu.SemaphoreType.DMA((8,))],
        flops=5 * 10**8,
    )
    return gq, gk, gv


def solution(mesh):
    tokens = (*CHIP_BITS, "core")
    grid = Mesh(mesh.devices.reshape(2, 2, 2, 2, 2, 2, 4), (*tokens, "head"))
    rows = P(tokens, "head")
    return jax.shard_map(
        local,
        mesh=grid,
        in_specs=(rows, rows, rows, rows, P("head", tokens), P("head")),
        out_specs=(rows, rows, rows),
        check_vma=False,
    )
```
